32 devices in a mesh: groups: 2 (over x), mp: 16 (over z, y, core).
Axes of the slice: x: 2, y: 2, z: 4, core: 2. Of those that a mesh axis runs over, the one named last changes fastest.
Arguments:
- features: bfloat16 [32, 256, 128, 128], P(None, ('groups', 'mp')), parts along dimension 1, may hold values from -6 to 6
- cotangent: bfloat16 [32, 256, 128, 128], P(None, ('groups', 'mp')), parts along dimension 1, may hold values from -9 to 9
- spectral_weight: float32 [256, 2, 16, 32, 32], P('mp'), may hold values from -9 to 9
- pointwise_weight: bfloat16 [32, 32], replicated, may hold values from -1 to 1
- biases: float32 [32], replicated, may hold values from -3 to 3
Outputs:
- features_grad: bfloat16 [32, 256, 128, 128], P(None, ('groups', 'mp')), parts along dimension 1
- spectral_grad: float32 [512, 2, 16, 32, 32], P(('groups', 'mp')), parts along dimension 0
- pointwise_grad: float32 [64, 32], P('groups'), parts along dimension 0
- biases_grad: float32 [64], P('groups'), parts along dimension 0
The draws below stay inside these ranges and needn't reach their ends.
There are 2 independent parts, one for each index of `groups`. The reference program is written for one: setup_inputs(seed, part) draws one part's arguments, and reference() takes and returns one part's arrays. A program takes and returns all parts, laid end to end along the dimension named above; an argument that names none is the same for every part. Nothing has to cross between parts.
All inputs are finite; a program needn't handle non-finite values.
Results may differ from the reference program's by a relative error of at most 0.007.
Values sent between devices are 32-bit elements; how exact they have to be, the bound alone decides.
No kernel may reach another device: no remote copies, remote signals or barrier semaphores. Data moves between devices by JAX's collectives and lax.ppermute only.
A program may use at most 128 MiB of HBM per device.

```python
import math
import jax
import jax.numpy as jnp
from jax import lax

C = 32
NX = 128
NY = 128
NZ = 128
KX = 16
KY = 16
KZ = 16
PAIRS = 256


def draw_cotangent(key, part):
    ramp = 0.5 + jnp.arange(NX, dtype=jnp.float32) * (1.0 / (NX - 1))
    base = jnp.clip(jax.random.normal(key, (C, NX, NY, NZ), jnp.float32), -5.5, 5.5)
    return (base * ramp[None, :, None, None]).astype(jnp.bfloat16)


def shard_levels(key, shape, pieces, smallest, largest):
    loudness = 1.0
    for dim, shards_of in pieces:
        steps = jax.random.uniform(jax.random.fold_in(jax.random.fold_in(key, 6), dim), (shards_of,), jnp.float32, smallest / len(pieces), largest / len(pieces))
        loudness = loudness * jnp.repeat(jnp.exp(steps), shape[dim] // shards_of).reshape((-1,) + (1,) * (len(shape) - 1 - dim))
    return loudness


def gaussian(key, dims, deviation, reach, cuts=(), kind=jnp.bfloat16):
    result = jax.random.normal(key, dims, jnp.float32) * deviation
    if len(cuts) > 0:
        result = shard_levels(key, dims, cuts, -0.22, 0.18) * result
    return jnp.clip(result, min=-reach, max=reach).astype(kind)


def setup_inputs(seed: int = 0, part: int = 0) -> dict:
    seeds = jax.random.split(jax.random.key(seed), 6)
    own_keys = jax.random.split(jax.random.fold_in(seeds[5], part), 6)
    return {
        "features": gaussian(own_keys[0], (C, NX, NY, NZ), 1.0, 6.0, ((1, 16),)),
        "cotangent": draw_cotangent(jax.random.fold_in(jax.random.fold_in(seeds[5], part), 71), part),
        "spectral_weight": gaussian(seeds[2], (PAIRS, 2, KX, C, C), 1.5, 9.0, ((0, 16),), jnp.float32),
        "pointwise_weight": gaussian(seeds[3], (C, C), C ** -0.5, 1.0),
        "biases": gaussian(seeds[4], (C,), 0.5, 3.0, (), jnp.float32),
    }


precise = lax.Precision.HIGHEST

def axis_tables(length, mode_count, signed):
    freqs = jnp.arange(mode_count, dtype=jnp.int32) - (mode_count // 2 if signed else 0)
    spots = jnp.arange(length, dtype=jnp.int32)
    phases = (spots[:, None] * freqs[None, :] % length).astype(jnp.float32) * (2.0 * math.pi / length)
    return (jnp.cos(phases), jnp.sin(phases))

def spectrum_plane(data, z_cos, z_sin, y_cos, y_sin, z_scale):
    hold = data.astype(jnp.float32)
    z_real = jnp.einsum('cxyz,zk->kcxy', hold, z_cos, precision=precise) * z_scale[:, None, None, None]
    z_imag = -jnp.einsum('cxyz,zk->kcxy', hold, z_sin, precision=precise) * z_scale[:, None, None, None]
    y_real = jnp.einsum('kcxy,yj->jkcx', z_real, y_cos, precision=precise) + jnp.einsum('kcxy,yj->jkcx', z_imag, y_sin, precision=precise)
    y_imag = jnp.einsum('kcxy,yj->jkcx', z_imag, y_cos, precision=precise) - jnp.einsum('kcxy,yj->jkcx', z_real, y_sin, precision=precise)
    stacked = jnp.stack([y_real, y_imag], axis=2)
    return stacked.reshape(KY * KZ, 2, stacked.shape[3], stacked.shape[4])

def spectrum_lines(part, x_cos, x_sin):
    a_real = part[:, 0]
    a_imag = part[:, 1]
    v_real = jnp.einsum('pcx,xk->pck', a_real, x_cos, precision=precise) + jnp.einsum('pcx,xk->pck', a_imag, x_sin, precision=precise)
    v_imag = jnp.einsum('pcx,xk->pck', a_imag, x_cos, precision=precise) - jnp.einsum('pcx,xk->pck', a_real, x_sin, precision=precise)
    return jnp.stack([v_real, v_imag], axis=1)

def space_lines(spec, x_cos, x_sin):
    u_real = spec[:, 0]
    u_imag = spec[:, 1]
    b_real = jnp.einsum('pck,xk->pcx', u_real, x_cos, precision=precise) - jnp.einsum('pck,xk->pcx', u_imag, x_sin, precision=precise)
    b_imag = jnp.einsum('pck,xk->pcx', u_imag, x_cos, precision=precise) + jnp.einsum('pck,xk->pcx', u_real, x_sin, precision=precise)
    return jnp.stack([b_real, b_imag], axis=1)

def space_plane(stacked, y_cos, y_sin, z_cos, z_sin):
    grid = stacked.reshape(KY, KZ, 2, stacked.shape[2], stacked.shape[3])
    q_real = grid[:, :, 0]
    q_imag = grid[:, :, 1]
    b_real = jnp.einsum('jkcx,yj->kcxy', q_real, y_cos, precision=precise) - jnp.einsum('jkcx,yj->kcxy', q_imag, y_sin, precision=precise)
    b_imag = jnp.einsum('jkcx,yj->kcxy', q_imag, y_cos, precision=precise) + jnp.einsum('jkcx,yj->kcxy', q_real, y_sin, precision=precise)
    return jnp.einsum('kcxy,zk->cxyz', b_real, z_cos, precision=precise) - jnp.einsum('kcxy,zk->cxyz', b_imag, z_sin, precision=precise)

def modes_product(spec, weight):
    v_real, v_imag = (spec[:, 0], spec[:, 1])
    r_real, r_imag = (weight[:, 0], weight[:, 1])
    u_real = jnp.einsum('pck,pkco->pok', v_real, r_real, precision=precise) - jnp.einsum('pck,pkco->pok', v_imag, r_imag, precision=precise)
    u_imag = jnp.einsum('pck,pkco->pok', v_real, r_imag, precision=precise) + jnp.einsum('pck,pkco->pok', v_imag, r_real, precision=precise)
    return jnp.stack([u_real, u_imag], axis=1)

def modes_adjoint(dspec, weight):
    d_real, d_imag = (dspec[:, 0], dspec[:, 1])
    r_real, r_imag = (weight[:, 0], weight[:, 1])
    g_real = jnp.einsum('pok,pkco->pck', d_real, r_real, precision=precise) + jnp.einsum('pok,pkco->pck', d_imag, r_imag, precision=precise)
    g_imag = jnp.einsum('pok,pkco->pck', d_imag, r_real, precision=precise) - jnp.einsum('pok,pkco->pck', d_real, r_imag, precision=precise)
    return jnp.stack([g_real, g_imag], axis=1)

def modes_gradient(spec, dspec):
    v_real, v_imag = (spec[:, 0], spec[:, 1])
    d_real, d_imag = (dspec[:, 0], dspec[:, 1])
    w_real = jnp.einsum('pck,pok->pkco', v_real, d_real, precision=precise) + jnp.einsum('pck,pok->pkco', v_imag, d_imag, precision=precise)
    w_imag = jnp.einsum('pck,pok->pkco', v_real, d_imag, precision=precise) - jnp.einsum('pck,pok->pkco', v_imag, d_real, precision=precise)
    return jnp.stack([w_real, w_imag], axis=1)

def reference(features, cotangent, spectral_weight, pointwise_weight, biases):
    z_cos, z_sin = axis_tables(NZ, KZ, False)
    z_cos = lax.optimization_barrier(z_cos.astype(jnp.bfloat16)).astype(jnp.float32)
    z_sin = lax.optimization_barrier(z_sin.astype(jnp.bfloat16)).astype(jnp.float32)
    y_cos, y_sin = axis_tables(NY, KY, True)
    x_cos, x_sin = axis_tables(NX, KX, True)
    z_cos_full, z_sin_full = axis_tables(NZ, KZ, False)
    z_weight = jnp.where(jnp.arange(KZ) == 0, 1.0, 2.0).astype(jnp.float32) / float(NX * NY * NZ)
    unit_weight = jnp.ones((KZ,), jnp.float32)
    spec = spectrum_lines(spectrum_plane(features, z_cos, z_sin, y_cos, y_sin, unit_weight), x_cos, x_sin)
    mixed = modes_product(spec, spectral_weight)
    spectral = space_plane(space_lines(mixed, x_cos, x_sin), y_cos, y_sin, z_cos_full * z_weight[None, :], z_sin_full * z_weight[None, :])
    feats = features.astype(jnp.float32)
    mixer = pointwise_weight.astype(jnp.float32)
    preact = spectral + jnp.einsum('oc,cxyz->oxyz', mixer, feats, precision=precise) + biases[:, None, None, None]
    _, pullback = jax.vjp(jax.nn.gelu, preact)
    pre_grad = pullback(cotangent.astype(jnp.float32))[0].astype(jnp.bfloat16)
    dspec = spectrum_lines(spectrum_plane(pre_grad, z_cos, z_sin, y_cos, y_sin, z_weight), x_cos, x_sin)
    spectral_grad = modes_gradient(spec, dspec)
    dmixed = modes_adjoint(dspec, spectral_weight)
    grads_f = pre_grad.astype(jnp.float32)
    back = space_plane(space_lines(dmixed, x_cos, x_sin), y_cos, y_sin, z_cos_full, z_sin_full)
    features_grad = (back + jnp.einsum('oc,oxyz->cxyz', mixer, grads_f, precision=precise)).astype(jnp.bfloat16)
    factor = float(NX * NY * NZ) ** (-0.5)
    pointwise_grad = jnp.einsum('oxyz,cxyz->oc', grads_f, feats, precision=precise) * factor
    biases_grad = lax.optimization_barrier(jnp.sum(grads_f, axis=(1, 2, 3))) * factor
    return (features_grad, spectral_grad, pointwise_grad, biases_grad)
```

```python
import functools
import math

import jax
import jax.numpy as jnp
import ml_dtypes
import numpy as np
from jax import lax
from jax.experimental import pallas as pl
from jax.experimental.pallas import tpu as pltpu
from jax.sharding import PartitionSpec as P

KX = 16
KY = 16
KZ = 16
XB = 4
CB = 8
YB = 16
VMEM = 56 << 20

F32 = jnp.float32
BF16 = jnp.bfloat16


def angles(length, modes, signed):
    freqs = np.arange(modes) - (modes // 2 if signed else 0)
    theta = (np.arange(length)[:, None] * freqs[None, :] % length) * (2.0 * math.pi / length)
    return np.cos(theta), np.sin(theta)


def bf16(table):
    return np.asarray(table, np.float32).astype(ml_dtypes.bfloat16)


@functools.cache
def plane_tables(ny, nz):
    yc, ys = angles(ny, KY, True)
    zc, zs = angles(nz, KZ, False)
    eye_x = np.eye(XB)
    rows = np.stack([np.stack([yc, -ys], 0), np.stack([-ys, -yc], 0)], 0)
    y_in = np.einsum("mryj,xw->mjrxwy", rows, eye_x).reshape(2 * KY * 2 * XB, XB * ny)
    z_in = np.einsum("mzk,cd->cmzkd", np.stack([zc, zs], 0), np.eye(CB)).reshape(CB, 2 * nz, KZ * CB)
    mix = np.stack([np.stack([yc, -ys], 0), np.stack([ys, yc], 0)], 0)
    y_out = np.einsum("qryj,xw->xqyjrw", mix, eye_x).reshape(XB, 2 * ny, KY * 2 * XB)
    z_out = np.einsum("qzk,cd->qkcdz", np.stack([zc, -zs], 0), np.eye(CB)).reshape(2 * KZ * CB, CB * nz)
    return bf16(y_in), bf16(z_in), bf16(y_out), bf16(z_out)


@functools.cache
def line_tables(nx):
    xc, xs = angles(nx, KX, True)
    inward = np.stack([np.stack([xc, -xs], 1), np.stack([xs, xc], 1)], 0)
    outward = np.stack([np.stack([xc, -xs], 1), np.stack([xs, xc], 1)], 0)
    blocks = nx // XB

    def order(table):
        return (
            table.reshape(2, blocks, XB, 2 * KX)
            .transpose(1, 0, 2, 3)
            .reshape(nx * 2, 2 * KX)
            .astype(np.float32)
        )

    return order(inward), order(outward)


@functools.cache
def lane_tables(pairs, channels):
    groups = channels // CB
    perm = np.einsum("kl,gh,cd->kgchld", np.eye(pairs), np.eye(groups), np.eye(CB))
    return bf16(perm.reshape(pairs * channels, pairs * channels))


def params(**kw):
    return pltpu.CompilerParams(vmem_limit_bytes=VMEM, **kw)


def exact_dot(a, b, dims):
    return lax.dot_general(a, b, (dims, ((), ())), precision=lax.Precision.HIGHEST, preferred_element_type=F32)


def dot(a, b):
    return jnp.dot(a, b, preferred_element_type=F32)


def split3(v):
    hi = v.astype(BF16)
    rest = v - hi.astype(F32)
    mid = rest.astype(BF16)
    return hi, mid, (rest - mid.astype(F32)).astype(BF16)


def analyse_group(planes, y_in, z_in_ref):
    total = None
    for c in range(0, CB, 2):
        pair = jnp.concatenate([planes(c), planes(c + 1)], axis=1)
        nz = pair.shape[1] // 2
        g = dot(y_in, pair).astype(BF16)
        half = g.shape[0] // 2
        for i in range(2):
            lhs = jnp.concatenate([g[:half, i * nz : (i + 1) * nz], g[half:, i * nz : (i + 1) * nz]], axis=1)
            term = dot(lhs, z_in_ref[c + i])
            total = term if total is None else total + term
    return total


def lines_kernel(f_ref, y_in_ref, z_in_ref, out_ref):
    y_in = y_in_ref[...]
    total = analyse_group(lambda c: f_ref[c].reshape(-1, f_ref.shape[-1]), y_in, z_in_ref)
    out_ref[:, 0] = total.reshape(out_ref.shape[0], 2 * XB, total.shape[1])


def feature_lines(features):
    channels, rows, ny, nz = features.shape
    y_in, z_in, _, _ = plane_tables(ny, nz)
    blocks = rows // XB
    return pl.pallas_call(
        lines_kernel,
        grid=(blocks, channels // CB),
        in_specs=[
            pl.BlockSpec((CB, XB, ny, nz), lambda h, g: (g, h, 0, 0)),
            pl.BlockSpec(y_in.shape, lambda h, g: (0, 0)),
            pl.BlockSpec(z_in.shape, lambda h, g: (0, 0, 0)),
        ],
        out_specs=pl.BlockSpec((KY, 1, 2 * XB, KZ * CB), lambda h, g: (0, h, 0, g)),
        out_shape=jax.ShapeDtypeStruct((KY, blocks, 2 * XB, KZ * channels), F32),
        compiler_params=params(),
        name="feature_lines",
    )(features, jnp.asarray(y_in), jnp.asarray(z_in))


def mix_kernel(scale_ref, lines_ref, w_ref, x_in_ref, x_out_ref, perm_ref, out_ref, spec_ref, rows_ref):
    k = pl.program_id(0)
    pairs = pl.num_programs(0)
    channels = w_ref.shape[-1]
    groups = channels // CB
    lanes = lines_ref.shape[1]
    per_group = lanes // groups

    @pl.when(k == 0)
    def _():
        spec_ref[...] = exact_dot(lines_ref[...].T, x_in_ref[...], ((1,), (0,)))

    v = jnp.concatenate(
        [spec_ref[pl.ds(pl.multiple_of(g * per_group + k * CB, CB), CB), :] for g in range(groups)], axis=0
    )
    reals, imags = [], []
    for a in range(KX):
        vr, vi = v[:, a : a + 1], v[:, KX + a : KX + a + 1]
        wr, wi = w_ref[0, 0, a], w_ref[0, 1, a]
        reals.append(jnp.sum(vr * wr - vi * wi, axis=0, keepdims=True))
        imags.append(jnp.sum(vr * wi + vi * wr, axis=0, keepdims=True))
    rows_ref[k] = jnp.concatenate(reals + imags, axis=0)

    @pl.when(k == pairs - 1)
    def _():
        mixed = jnp.concatenate([rows_ref[i] for i in range(rows_ref.shape[0])], axis=1)
        parts = dot(jnp.concatenate(split3(mixed), axis=0), perm_ref[...])
        n = mixed.shape[0]
        placed = (parts[2 * n :] + parts[n : 2 * n]) + parts[:n]
        out_ref[...] = exact_dot(x_out_ref[...], placed * scale_ref[...], ((1,), (0,)))


def whole(shape):
    return pl.BlockSpec(shape, lambda k: (0,) * len(shape))


def mix_modes(lines, weight, scale, x_in, x_out, perm):
    pairs, _, kx, channels, _ = weight.shape
    lanes = pairs * channels
    return pl.pallas_call(
        mix_kernel,
        grid=(pairs,),
        in_specs=[
            whole(scale.shape),
            whole(lines.shape),
            pl.BlockSpec((1, 2, kx, channels, channels), lambda k: (k, 0, 0, 0, 0)),
            whole(x_in.shape),
            whole(x_out.shape),
            whole(perm.shape),
        ],
        out_specs=[whole(lines.shape), whole((lanes, 2 * kx))],
        out_shape=[jax.ShapeDtypeStruct(lines.shape, F32), jax.ShapeDtypeStruct((lanes, 2 * kx), F32)],
        scratch_shapes=[pltpu.VMEM((pairs, 2 * kx, channels), F32)],
        compiler_params=params(),
        name="mix_modes",
    )(scale, lines, weight, x_in, x_out, perm)


def adjoint_kernel(scale_ref, lines_ref, w_ref, x_in_ref, x_out_ref, perm_ref, out_ref, dspec_ref, cols_ref):
    k = pl.program_id(0)
    pairs = pl.num_programs(0)
    channels = w_ref.shape[-1]
    groups = channels // CB
    lanes = lines_ref.shape[1]
    per_group = lanes // groups

    @pl.when(k == 0)
    def _():
        placed = exact_dot(x_in_ref[...].T, lines_ref[...], ((1,), (0,))) * scale_ref[...]
        n = placed.shape[0]
        parts = lax.dot_general(
            jnp.concatenate(split3(placed), axis=0), perm_ref[...], (((1,), (0,)), ((), ())), preferred_element_type=F32
        )
        rows = (parts[2 * n :] + parts[n : 2 * n]) + parts[:n]
        for i in range(dspec_ref.shape[0]):
            dspec_ref[i] = rows[:, i * channels : (i + 1) * channels]

    d = dspec_ref[k]
    lane = lax.broadcasted_iota(jnp.int32, (channels, 2 * KX), 1)
    cols = jnp.zeros((channels, 2 * KX), F32)
    for a in range(KX):
        dr, di = d[a : a + 1], d[KX + a : KX + a + 1]
        wr, wi = w_ref[0, 0, a], w_ref[0, 1, a]
        cols = jnp.where(lane == a, jnp.sum(dr * wr + di * wi, axis=1, keepdims=True), cols)
        cols = jnp.where(lane == KX + a, jnp.sum(di * wr - dr * wi, axis=1, keepdims=True), cols)
    for g in range(groups):
        cols_ref[pl.ds(pl.multiple_of(g * per_group + k * CB, CB), CB), :] = cols[g * CB : (g + 1) * CB]

    @pl.when(k == pairs - 1)
    def _():
        out_ref[...] = exact_dot(x_out_ref[...], cols_ref[...], ((1,), (1,)))


def adjoint_modes(lines, weight, scale, x_in, x_out, perm_back):
    pairs, _, kx, channels, _ = weight.shape
    lanes = pairs * channels
    return pl.pallas_call(
        adjoint_kernel,
        grid=(pairs,),
        in_specs=[
            whole(scale.shape),
            whole(lines.shape),
            pl.BlockSpec((1, 2, kx, channels, channels), lambda k: (k, 0, 0, 0, 0)),
            whole(x_in.shape),
            whole(x_out.shape),
            whole(perm_back.shape),
        ],
        out_specs=[whole(lines.shape), whole((pairs, 2 * kx, channels))],
        out_shape=[jax.ShapeDtypeStruct(lines.shape, F32), jax.ShapeDtypeStruct((pairs, 2 * kx, channels), F32)],
        scratch_shapes=[pltpu.VMEM((lanes, 2 * kx), F32)],
        compiler_params=params(),
        name="adjoint_modes",
    )(scale, lines, weight, x_in, x_out, perm_back)


def outer_kernel(spec_ref, dspec_ref, out_ref):
    k = pl.program_id(0)
    channels = dspec_ref.shape[-1]
    groups = channels // CB
    per_group = spec_ref.shape[0] // groups
    v = jnp.concatenate(
        [spec_ref[pl.ds(pl.multiple_of(g * per_group + k * CB, CB), CB), :] for g in range(groups)], axis=0
    )
    d = dspec_ref[0]
    for a in range(KX):
        vr, vi = v[:, a : a + 1], v[:, KX + a : KX + a + 1]
        dr, di = d[a : a + 1], d[KX + a : KX + a + 1]
        out_ref[0, 0, a] = vr * dr + vi * di
        out_ref[0, 1, a] = vr * di - vi * dr


def mode_gradient(spec, dspec):
    pairs, twice_kx, channels = dspec.shape
    shape = (pairs, 2, twice_kx // 2, channels, channels)
    return pl.pallas_call(
        outer_kernel,
        grid=(pairs,),
        in_specs=[whole(spec.shape), pl.BlockSpec((1, twice_kx, channels), lambda k: (k, 0, 0))],
        out_specs=pl.BlockSpec((1,) + shape[1:], lambda k: (k, 0, 0, 0, 0)),
        out_shape=jax.ShapeDtypeStruct(shape, F32),
        compiler_params=params(),
        name="mode_gradient",
    )(spec, dspec)


def synthesise(x, lines_ref, y_out_ref, z_out_ref, low_ref, b_ref, space_ref):
    within = lax.rem(x, XB)
    rows = KY * 2 * XB

    @pl.when(within == 0)
    def _():
        block = lines_ref[:, 0].reshape(rows, lines_ref.shape[-1])
        hi = block.astype(BF16)
        low_ref[:rows] = hi
        low_ref[rows:] = (block - hi.astype(F32)).astype(BF16)

    table = y_out_ref[within]
    b_ref[...] = dot(jnp.concatenate([table, table], axis=1), low_ref[...]).astype(BF16)
    ny = table.shape[0] // 2
    lanes = KZ * CB
    for g in range(space_ref.shape[0]):
        lhs = jnp.concatenate([b_ref[:ny, g * lanes : (g + 1) * lanes], b_ref[ny:, g * lanes : (g + 1) * lanes]], axis=1)
        space_ref[g] = dot(lhs, z_out_ref[...])


def channel_mix(kron, cells_ref, y):
    nz = cells_ref.shape[-1]
    tiles = [cells_ref[:, 0, y + t * YB : y + (t + 1) * YB, :].reshape(-1, nz) for t in range(2)]
    return dot(kron, jnp.concatenate(tiles, axis=1))


ROOT = math.sqrt(2.0 / math.pi)
CUBE = 0.044715 * ROOT


def gelu_slope(u):
    square = u * u
    t = jnp.tanh(u * (ROOT + CUBE * square))
    inner = u * (0.5 * ROOT + 1.5 * CUBE * square)
    return (1.0 + t) * (0.5 + (1.0 - t) * inner)


def slope_kernel(
    bias_ref, lines_ref, f_ref, cot_ref, kron_ref, y_in_ref, z_in_ref, y_out_ref, z_out_ref,
    grad_ref, out_ref, low_ref, b_ref, space_ref, keep_ref,
):
    x = pl.program_id(0)
    within = lax.rem(x, XB)
    channels, _, ny, nz = f_ref.shape
    synthesise(x, lines_ref, y_out_ref, z_out_ref, low_ref, b_ref, space_ref)
    for y in range(0, ny, 2 * YB):
        local = channel_mix(kron_ref[...], f_ref, y)
        for o in range(channels):
            g, c = divmod(o, CB)
            for t in range(2):
                first = y + t * YB
                u = (
                    space_ref[g, first : first + YB, c * nz : (c + 1) * nz]
                    + local[o * YB : (o + 1) * YB, t * nz : (t + 1) * nz]
                    + bias_ref[o]
                )
                grad = (gelu_slope(u) * cot_ref[o, 0, first : first + YB, :].astype(F32)).astype(BF16)
                grad_ref[o, 0, first : first + YB, :] = grad
                keep_ref[o, pl.ds(pl.multiple_of(within * ny + first, YB), YB), :] = grad

    @pl.when(within == XB - 1)
    def _():
        y_in = y_in_ref[...]
        lanes = KZ * CB
        for g in range(channels // CB):
            total = analyse_group(lambda c: keep_ref[g * CB + c], y_in, z_in_ref)
            out_ref[:, 0, :, g * lanes : (g + 1) * lanes] = total.reshape(out_ref.shape[0], 2 * XB, lanes)


def cells_specs(channels, ny, nz):
    return pl.BlockSpec((channels, 1, ny, nz), lambda x: (0, x, 0, 0))


def slope(lines, features, cotangent, kron, biases):
    channels, rows, ny, nz = features.shape
    y_in, z_in, y_out, z_out = plane_tables(ny, nz)
    blocks = rows // XB
    lanes = KZ * channels
    line_spec = pl.BlockSpec((KY, 1, 2 * XB, lanes), lambda x: (0, x // XB, 0, 0))
    cells = cells_specs(channels, ny, nz)
    return pl.pallas_call(
        slope_kernel,
        grid=(rows,),
        in_specs=[
            pl.BlockSpec(memory_space=pltpu.SMEM),
            line_spec,
            cells,
            cells,
            whole(kron.shape),
            whole(y_in.shape),
            whole(z_in.shape),
            whole(y_out.shape),
            whole(z_out.shape),
        ],
        out_specs=[cells, line_spec],
        out_shape=[
            jax.ShapeDtypeStruct(features.shape, BF16),
            jax.ShapeDtypeStruct((KY, blocks, 2 * XB, lanes), F32),
        ],
        scratch_shapes=[
            pltpu.VMEM((2 * KY * 2 * XB, lanes), BF16),
            pltpu.VMEM((2 * ny, lanes), BF16),
            pltpu.VMEM((channels // CB, ny, CB * nz), F32),
            pltpu.VMEM((channels, XB * ny, nz), BF16),
        ],
        compiler_params=params(),
        name="slope",
    )(biases, lines, features, cotangent, kron, jnp.asarray(y_in), jnp.asarray(z_in), jnp.asarray(y_out), jnp.asarray(z_out))


def back_kernel(lines_ref, grad_ref, kron_ref, y_out_ref, z_out_ref, out_ref, low_ref, b_ref, space_ref):
    x = pl.program_id(0)
    channels, _, ny, nz = grad_ref.shape
    synthesise(x, lines_ref, y_out_ref, z_out_ref, low_ref, b_ref, space_ref)
    for y in range(0, ny, 2 * YB):
        local = channel_mix(kron_ref[...], grad_ref, y)
        for o in range(channels):
            g, c = divmod(o, CB)
            for t in range(2):
                first = y + t * YB
                u = (
                    space_ref[g, first : first + YB, c * nz : (c + 1) * nz]
                    + local[o * YB : (o + 1) * YB, t * nz : (t + 1) * nz]
                )
                out_ref[o, 0, first : first + YB, :] = u.astype(BF16)


def back(lines, pre_grad, kron):
    channels, rows, ny, nz = pre_grad.shape
    _, _, y_out, z_out = plane_tables(ny, nz)
    lanes = KZ * channels
    cells = cells_specs(channels, ny, nz)
    return pl.pallas_call(
        back_kernel,
        grid=(rows,),
        in_specs=[
            pl.BlockSpec((KY, 1, 2 * XB, lanes), lambda x: (0, x // XB, 0, 0)),
            cells,
            whole(kron.shape),
            whole(y_out.shape),
            whole(z_out.shape),
        ],
        out_specs=cells,
        out_shape=jax.ShapeDtypeStruct(pre_grad.shape, BF16),
        scratch_shapes=[
            pltpu.VMEM((2 * KY * 2 * XB, lanes), BF16),
            pltpu.VMEM((2 * ny, lanes), BF16),
            pltpu.VMEM((channels // CB, ny, CB * nz), F32),
        ],
        compiler_params=params(),
        name="back",
    )(lines, pre_grad, kron, jnp.asarray(y_out), jnp.asarray(z_out))


def cell_sums_kernel(grad_ref, f_ref, out_ref, acc_ref, row_ref):
    x = pl.program_id(0)
    channels, _, ny, nz = f_ref.shape

    def tiles(ref):
        return jnp.concatenate([ref[:, 0, y : y + YB, :].reshape(-1, nz) for y in range(0, ny, YB)], axis=1)

    grads = tiles(grad_ref)
    term = lax.dot_general(grads, tiles(f_ref), (((1,), (1,)), ((), ())), preferred_element_type=F32)
    ones = jnp.ones((grads.shape[1], 128), BF16)
    sums = dot(grads, ones)

    @pl.when(x == 0)
    def _():
        acc_ref[...] = term
        row_ref[...] = sums

    @pl.when(x > 0)
    def _():
        acc_ref[...] += term
        row_ref[...] += sums

    @pl.when(x == pl.num_programs(0) - 1)
    def _():
        n = channels * YB
        same = lax.rem(lax.broadcasted_iota(jnp.int32, (n, n), 0), YB) == lax.rem(
            lax.broadcasted_iota(jnp.int32, (n, n), 1), YB
        )
        picked = jnp.where(same, acc_ref[...], 0.0)
        fold = (
            lax.broadcasted_iota(jnp.int32, (channels, n), 1) // YB
            == lax.broadcasted_iota(jnp.int32, (channels, n), 0)
        ).astype(F32)
        half = exact_dot(fold, picked, ((1,), (0,)))
        out_ref[0] = exact_dot(half, fold, ((1,), (1,)))
        out_ref[1] = exact_dot(fold, row_ref[...], ((1,), (0,)))[:, :channels]


def cell_sums(pre_grad, features):
    channels, rows, ny, nz = features.shape
    cells = cells_specs(channels, ny, nz)
    return pl.pallas_call(
        cell_sums_kernel,
        grid=(rows,),
        in_specs=[cells, cells],
        out_specs=whole((2, channels, channels)),
        out_shape=jax.ShapeDtypeStruct((2, channels, channels), F32),
        scratch_shapes=[pltpu.VMEM((channels * YB, channels * YB), F32), pltpu.VMEM((channels * YB, 128), F32)],
        compiler_params=params(),
        name="cell_sums",
    )(pre_grad, features)


def swap(blocks):
    return lax.all_to_all(blocks, "mp", 0, 0, tiled=True)


def shards(features, cotangent, spectral_weight, pointwise_weight, biases):
    channels, rows, ny, nz = features.shape
    devices = lax.axis_size("mp")
    nx = rows * devices
    pairs = spectral_weight.shape[0]
    groups = channels // CB
    blocks = rows // XB
    cut = KZ // pairs
    cells = nx * ny * nz
    x_in, x_out = (jnp.asarray(t) for t in line_tables(nx))
    perm = jnp.asarray(lane_tables(pairs, channels))
    perm_back = jnp.asarray(lane_tables(pairs, channels).T)
    if cut == 1:
        first_k = 0
    else:
        first_k = lax.rem(lax.axis_index("mp"), cut) * pairs
    ks = jnp.broadcast_to(jnp.arange(pairs)[None, :, None] + first_k, (groups, pairs, CB)).reshape(1, -1)
    scale = jnp.where(ks == 0, 1.0, 2.0).astype(F32) / float(cells)

    def to_owner(lines):
        if cut > 1:
            lines = lines.reshape(KY, blocks, 2 * XB, groups, cut, pairs * CB)
            lines = lines.transpose(0, 4, 1, 2, 3, 5)
        return swap(lines.reshape(devices, blocks, 2 * XB, -1)).reshape(nx * 2, -1)

    def to_cells(lines):
        lines = swap(lines.reshape(devices, blocks, 2 * XB, -1))
        if cut > 1:
            lines = lines.reshape(KY, cut, blocks, 2 * XB, groups, pairs * CB)
            lines = lines.transpose(0, 2, 3, 4, 1, 5)
        return lines.reshape(KY, blocks, 2 * XB, -1)

    eye = jnp.eye(YB, dtype=BF16)
    kron = jnp.kron(pointwise_weight, eye)
    kron_back = jnp.kron(pointwise_weight.T, eye)

    lines = to_owner(feature_lines(features))
    mixed, spec = mix_modes(lines, spectral_weight, scale, x_in, x_out, perm)
    pre_grad, dlines = slope(to_cells(mixed), features, cotangent, kron, biases)
    dmixed, dspec = adjoint_modes(to_owner(dlines), spectral_weight, scale, x_in, x_out, perm_back)
    sums = cell_sums(pre_grad, features)
    sums = jnp.concatenate([sums[0].reshape(-1), sums[1, :, 0], jnp.zeros((channels * 3,), F32)])
    sums = swap(jnp.broadcast_to(sums.reshape(1, -1, 128), (devices, sums.size // 128, 128)))
    total = jnp.sum(sums, axis=0).reshape(-1) * float(cells) ** -0.5
    mix_total = total[: channels * channels].reshape(channels, channels)
    bias_total = total[channels * channels : channels * channels + channels]
    features_grad = back(to_cells(dmixed), pre_grad, kron_back)
    spectral_grad = mode_gradient(spec, dspec)
    return (features_grad, spectral_grad, mix_total, bias_total)


def solution(mesh):
    return jax.shard_map(
        shards,
        mesh=mesh,
        in_specs=(
            P(None, ("groups", "mp"), None, None),
            P(None, ("groups", "mp"), None, None),
            P("mp", None, None, None, None),
            P(),
            P(),
        ),
        out_specs=(
            P(None, ("groups", "mp"), None, None),
            P(("groups", "mp"), None, None, None, None),
            P("groups", None),
            P("groups"),
        ),
        check_vma=False,
    )
```

```python
import functools
import math

import jax
import jax.numpy as jnp
import ml_dtypes
import numpy as np
from jax import lax
from jax.experimental import pallas as pl
from jax.experimental.pallas import tpu as pltpu
from jax.sharding import PartitionSpec as P

KX = 16
KY = 16
KZ = 16
XB = 4
CB = 8
YB = 16
MIB = 1 << 20

F32 = jnp.float32
BF16 = jnp.bfloat16


def angles(length, modes, signed):
    freqs = np.arange(modes) - (modes // 2 if signed else 0)
    theta = (np.arange(length)[:, None] * freqs[None, :] % length) * (2.0 * math.pi / length)
    return np.cos(theta), np.sin(theta)


def bf16(table):
    return np.asarray(table, np.float32).astype(ml_dtypes.bfloat16)


@functools.cache
def plane_tables(ny, nz):
    yc, ys = angles(ny, KY, True)
    zc, zs = angles(nz, KZ, False)
    eye_x = np.eye(XB)
    rows = np.stack([np.stack([yc, -ys], 0), np.stack([-ys, -yc], 0)], 0)
    y_in = np.einsum("mryj,xw->mjrxwy", rows, eye_x).reshape(2 * KY * 2 * XB, XB * ny)
    z_in = np.einsum("mzk,cd->cmzkd", np.stack([zc, zs], 0), np.eye(CB)).reshape(CB, 2 * nz, KZ * CB)
    mix = np.stack([np.stack([yc, -ys], 0), np.stack([ys, yc], 0)], 0)
    y_out = np.einsum("qryj,xw->xqyjrw", mix, eye_x).reshape(XB, 2 * ny, KY * 2 * XB)
    z_out = np.einsum("qzk,cd->qkcdz", np.stack([zc, -zs], 0), np.eye(CB)).reshape(2 * KZ * CB, CB * nz)
    return bf16(y_in), bf16(z_in), bf16(y_out), bf16(z_out)


@functools.cache
def line_tables(nx):
    xc, xs = angles(nx, KX, True)
    inward = np.stack([np.stack([xc, -xs], 1), np.stack([xs, xc], 1)], 0)
    outward = np.stack([np.stack([xc, -xs], 1), np.stack([xs, xc], 1)], 0)
    blocks = nx // XB

    def order(table):
        return (
            table.reshape(2, blocks, XB, 2 * KX)
            .transpose(1, 0, 2, 3)
            .reshape(nx * 2, 2 * KX)
            .astype(np.float32)
        )

    return order(inward), order(outward)


@functools.cache
def lane_tables(pairs, channels):
    groups = channels // CB
    perm = np.einsum("kl,gh,cd->kgchld", np.eye(pairs), np.eye(groups), np.eye(CB))
    return bf16(perm.reshape(pairs * channels, pairs * channels))


def params(mib):
    return pltpu.CompilerParams(vmem_limit_bytes=mib * MIB)


def exact_dot(a, b, dims):
    return lax.dot_general(a, b, (dims, ((), ())), precision=lax.Precision.HIGHEST, preferred_element_type=F32)


def dot(a, b):
    return jnp.dot(a, b, preferred_element_type=F32)


def split3(v):
    hi = v.astype(BF16)
    rest = v - hi.astype(F32)
    mid = rest.astype(BF16)
    return hi, mid, (rest - mid.astype(F32)).astype(BF16)


def analyse_y(planes, first, count, y_in, g_ref):
    rows = y_in.shape[0] // 2
    for c in range(first, first + count, 2):
        pair = jnp.concatenate([planes(c), planes(c + 1)], axis=1)
        nz = pair.shape[1] // 2
        g = dot(y_in, pair).astype(BF16)
        for i in range(2):
            group, of_group = divmod(c + i, CB)
            for m in range(2):
                g_ref[group * rows : (group + 1) * rows, (2 * of_group + m) * nz : (2 * of_group + m + 1) * nz] = g[
                    m * rows : (m + 1) * rows, i * nz : (i + 1) * nz
                ]


def analyse_z(z_in_ref, g_ref):
    return dot(g_ref[...], z_in_ref[...].reshape(g_ref.shape[1], -1))


def put_lines(out_ref, h, first_group, total):
    rows, lanes = KY * 2 * XB, total.shape[1]
    for g in range(total.shape[0] // rows):
        first = (first_group + g) * lanes
        out_ref[:, h, :, first : first + lanes] = total[g * rows : (g + 1) * rows].reshape(KY, 2 * XB, lanes)


def in_hbm():
    return pl.BlockSpec(memory_space=pltpu.HBM)


def in_vmem():
    return pl.BlockSpec(memory_space=pltpu.VMEM)


DEPTH = 3
PER_COPY = 4
PER_DOT = 16


def lines_kernel(f_hbm, y_in_hbm, z_in_hbm, out_ref, f_ref, g_ref, y_in_ref, z_in_ref, sem, table_sem):
    channels, rows, ny, nz = f_ref.shape
    copies = [
        pltpu.make_async_copy(f_hbm.at[pl.ds(c, PER_COPY)], f_ref.at[pl.ds(c, PER_COPY)], sem.at[c // PER_COPY])
        for c in range(0, channels, PER_COPY)
    ]
    tables = [
        pltpu.make_async_copy(y_in_hbm, y_in_ref, table_sem.at[0]),
        pltpu.make_async_copy(z_in_hbm, z_in_ref, table_sem.at[1]),
    ]
    tables[0].start()
    for copy in copies[:DEPTH]:
        copy.start()
    tables[1].start()
    tables[0].wait()
    y_in = y_in_ref[...]
    for first in range(0, channels, PER_DOT):
        for c in range(0, PER_DOT, PER_COPY):
            n = (first + c) // PER_COPY
            copies[n].wait()
            if n + DEPTH < len(copies):
                copies[n + DEPTH].start()
            for h in range(rows // XB):
                analyse_y(
                    lambda i: f_ref[first + i, h * XB : (h + 1) * XB].reshape(XB * ny, nz), c, PER_COPY, y_in, g_ref.at[h]
                )
        if first == 0:
            tables[1].wait()
        for h in range(rows // XB):
            put_lines(out_ref, h, first // CB, analyse_z(z_in_ref, g_ref.at[h]))


def feature_lines(features):
    channels, rows, ny, nz = features.shape
    y_in, z_in, _, _ = plane_tables(ny, nz)
    blocks = rows // XB
    return pl.pallas_call(
        lines_kernel,
        in_specs=[in_hbm()] * 3,
        out_specs=in_vmem(),
        out_shape=jax.ShapeDtypeStruct((KY, blocks, 2 * XB, KZ * channels), F32),
        scratch_shapes=[
            pltpu.VMEM(features.shape, BF16),
            pltpu.VMEM((blocks, PER_DOT // CB * KY * 2 * XB, CB * 2 * nz), BF16),
            pltpu.VMEM(y_in.shape, BF16),
            pltpu.VMEM(z_in.shape, BF16),
            pltpu.SemaphoreType.DMA((channels // PER_COPY,)),
            pltpu.SemaphoreType.DMA((2,)),
        ],
        compiler_params=params(60),
        name="feature_lines",
    )(features, jnp.asarray(y_in), jnp.asarray(z_in))


WEIGHT_DEPTH = 16


def columns(spec_ref, k, pairs, channels):
    groups = channels // CB
    per_group = pairs * CB
    return jnp.concatenate(
        [spec_ref[pl.ds(pl.multiple_of(g * per_group + k * CB, CB), CB), :] for g in range(groups)], axis=0
    )


def weight_copies(w_hbm, w_ref, sem):
    pairs = w_ref.shape[0]

    def copy(k):
        return pltpu.make_async_copy(w_hbm.at[k], w_ref.at[k], sem.at[k])

    for k in range(min(WEIGHT_DEPTH, pairs)):
        copy(k).start()

    def arrive(k):
        copy(k).wait()

        @pl.when(k + WEIGHT_DEPTH < pairs)
        def _():
            copy(k + WEIGHT_DEPTH).start()

    return arrive


def mix_kernel(scale_ref, lines_ref, w_hbm, x_in_ref, x_out_ref, perm_ref, out_ref, spec_ref, rows_ref, w_ref, sem):
    pairs, _, _, channels, _ = w_ref.shape
    arrive = weight_copies(w_hbm, w_ref, sem)
    spec_ref[...] = exact_dot(lines_ref[...].reshape(x_in_ref.shape[0], -1).T, x_in_ref[...], ((1,), (0,)))

    def step(k, carry):
        arrive(k)
        v = columns(spec_ref, k, pairs, channels)
        reals, imags = [], []
        for a in range(KX):
            vr, vi = v[:, a : a + 1], v[:, KX + a : KX + a + 1]
            wr, wi = w_ref[k, 0, a], w_ref[k, 1, a]
            reals.append(jnp.sum(vr * wr - vi * wi, axis=0, keepdims=True))
            imags.append(jnp.sum(vr * wi + vi * wr, axis=0, keepdims=True))
        rows_ref[k] = jnp.concatenate(reals + imags, axis=0)
        return carry

    lax.fori_loop(0, pairs, step, 0)
    mixed = jnp.concatenate([rows_ref[i] for i in range(pairs)], axis=1)
    parts = dot(jnp.concatenate(split3(mixed), axis=0), perm_ref[...])
    n = mixed.shape[0]
    placed = (parts[2 * n :] + parts[n : 2 * n]) + parts[:n]
    out_ref[...] = exact_dot(x_out_ref[...], placed * scale_ref[...], ((1,), (0,))).reshape(out_ref.shape)


def whole(shape):
    return pl.BlockSpec(shape, lambda k: (0,) * len(shape))


def mix_modes(lines, weight, scale, x_in, x_out, perm):
    pairs, _, kx, channels, _ = weight.shape
    lanes = pairs * channels
    return pl.pallas_call(
        mix_kernel,
        in_specs=[in_vmem(), in_vmem(), in_hbm(), in_vmem(), in_vmem(), in_vmem()],
        out_specs=[in_vmem(), in_vmem()],
        out_shape=[jax.ShapeDtypeStruct(lines.shape, F32), jax.ShapeDtypeStruct((lanes, 2 * kx), F32)],
        scratch_shapes=[
            pltpu.VMEM((pairs, 2 * kx, channels), F32),
            pltpu.VMEM(weight.shape, F32),
            pltpu.SemaphoreType.DMA((pairs,)),
        ],
        compiler_params=params(53),
        name="mix_modes",
    )(scale, lines, weight, x_in, x_out, perm)


def adjoint_kernel(scale_ref, lines_ref, w_hbm, x_in_ref, x_out_ref, perm_ref, out_ref, dspec_ref, cols_ref, w_ref, sem):
    pairs, _, _, channels, _ = w_ref.shape
    arrive = weight_copies(w_hbm, w_ref, sem)
    placed = exact_dot(x_in_ref[...].T, lines_ref[...].reshape(x_in_ref.shape[0], -1), ((1,), (0,))) * scale_ref[...]
    n = placed.shape[0]
    parts = dot(jnp.concatenate(split3(placed), axis=0), perm_ref[...])
    rows = (parts[2 * n :] + parts[n : 2 * n]) + parts[:n]
    for i in range(pairs):
        dspec_ref[i] = rows[:, i * channels : (i + 1) * channels]
    lane = lax.broadcasted_iota(jnp.int32, (channels, 2 * KX), 1)

    def step(k, carry):
        arrive(k)
        d = dspec_ref[k]
        cols = jnp.zeros((channels, 2 * KX), F32)
        for a in range(KX):
            dr, di = d[a : a + 1], d[KX + a : KX + a + 1]
            wr, wi = w_ref[k, 0, a], w_ref[k, 1, a]
            cols = jnp.where(lane == a, jnp.sum(dr * wr + di * wi, axis=1, keepdims=True), cols)
            cols = jnp.where(lane == KX + a, jnp.sum(di * wr - dr * wi, axis=1, keepdims=True), cols)
        for g in range(channels // CB):
            cols_ref[pl.ds(pl.multiple_of(g * pairs * CB + k * CB, CB), CB), :] = cols[g * CB : (g + 1) * CB]
        return carry

    lax.fori_loop(0, pairs, step, 0)
    out_ref[...] = exact_dot(x_out_ref[...], cols_ref[...], ((1,), (1,))).reshape(out_ref.shape)


def adjoint_modes(lines, weight, scale, x_in, x_out, perm_back):
    pairs, _, kx, channels, _ = weight.shape
    lanes = pairs * channels
    return pl.pallas_call(
        adjoint_kernel,
        in_specs=[in_vmem(), in_vmem(), in_hbm(), in_vmem(), in_vmem(), in_vmem()],
        out_specs=[in_vmem(), in_vmem()],
        out_shape=[jax.ShapeDtypeStruct(lines.shape, F32), jax.ShapeDtypeStruct((pairs, 2 * kx, channels), F32)],
        scratch_shapes=[
            pltpu.VMEM((lanes, 2 * kx), F32),
            pltpu.VMEM(weight.shape, F32),
            pltpu.SemaphoreType.DMA((pairs,)),
        ],
        compiler_params=params(53),
        name="adjoint_modes",
    )(scale, lines, weight, x_in, x_out, perm_back)


PER_STEP = 4


def outer_kernel(spec_ref, dspec_ref, out_ref):
    channels = dspec_ref.shape[-1]
    pairs = spec_ref.shape[0] // channels
    for i in range(PER_STEP):
        v = columns(spec_ref, pl.program_id(0) * PER_STEP + i, pairs, channels)
        d = dspec_ref[i]
        for a in range(KX):
            vr, vi = v[:, a : a + 1], v[:, KX + a : KX + a + 1]
            dr, di = d[a : a + 1], d[KX + a : KX + a + 1]
            out_ref[i, 0, a] = vr * dr + vi * di
            out_ref[i, 1, a] = vr * di - vi * dr


def mode_gradient(spec, dspec):
    pairs, twice_kx, channels = dspec.shape
    shape = (pairs, 2, twice_kx // 2, channels, channels)
    return pl.pallas_call(
        outer_kernel,
        grid=(pairs // PER_STEP,),
        in_specs=[whole(spec.shape), pl.BlockSpec((PER_STEP, twice_kx, channels), lambda k: (k, 0, 0))],
        out_specs=pl.BlockSpec((PER_STEP,) + shape[1:], lambda k: (k, 0, 0, 0, 0)),
        out_shape=jax.ShapeDtypeStruct(shape, F32),
        compiler_params=params(24),
        name="mode_gradient",
    )(spec, dspec)


def spread(w, by_column, out_ref):
    n = out_ref.shape[0]
    fold = (
        lax.broadcasted_iota(jnp.int32, (n, w.shape[0]), 0) // YB
        == lax.broadcasted_iota(jnp.int32, (n, w.shape[0]), 1)
    ).astype(F32).astype(BF16)
    wide = lax.dot_general(fold, w, (((1,), (1 if by_column else 0,)), ((), ())), preferred_element_type=F32)
    full = lax.dot_general(wide.astype(BF16), fold, (((1,), (1,)), ((), ())), preferred_element_type=F32)
    same = lax.rem(lax.broadcasted_iota(jnp.int32, (n, n), 0), YB) == lax.rem(
        lax.broadcasted_iota(jnp.int32, (n, n), 1), YB
    )
    out_ref[...] = jnp.where(same, full, 0.0).astype(BF16)


def synthesise_y(lines_ref, bias, y_out_ref, low_ref, b_ref):
    rows = KY * 2 * XB
    lanes = KZ * CB
    ny = b_ref.shape[2]
    tables = y_out_ref[...].reshape(-1, rows)
    tables = jnp.concatenate([tables, tables], axis=1)
    for h in range(lines_ref.shape[1]):
        block = lines_ref[:, h].reshape(rows, lines_ref.shape[-1])
        if bias is not None:
            row = lax.broadcasted_iota(jnp.int32, (rows, 1), 0) // XB
            block = block + jnp.where(row == KY // 2 * 2, bias, 0.0)
        hi = block.astype(BF16)
        low_ref[:rows] = hi
        low_ref[rows:] = (block - hi.astype(F32)).astype(BF16)
        b = dot(tables, low_ref[...]).astype(BF16)
        for x in range(XB):
            for part in range(2):
                first = (2 * x + part) * ny
                for g in range(b_ref.shape[1]):
                    b_ref[h * XB + x, g, :, part * lanes : (part + 1) * lanes] = b[
                        first : first + ny, g * lanes : (g + 1) * lanes
                    ]


def channel_mix(kron, cells_ref, x, y):
    nz = cells_ref.shape[-1]
    tiles = [cells_ref[:, x, y + t * YB : y + (t + 1) * YB, :].reshape(-1, nz) for t in range(2)]
    return dot(kron, jnp.concatenate(tiles, axis=1))


def store_mix(kron_ref, cells_ref, out_ref):
    channels, rows, ny, nz = cells_ref.shape
    for x in range(rows):
        for y in range(0, ny, 2 * YB):
            local = channel_mix(kron_ref[...], cells_ref, x, y).astype(BF16)
            for t in range(2):
                out_ref[:, x, y + t * YB : y + (t + 1) * YB, :] = local[:, t * nz : (t + 1) * nz].reshape(
                    channels, YB, nz
                )


def local_kernel(by_column, cells_ref, w_ref, out_ref, kron_ref):
    @pl.when(pl.program_id(0) == 0)
    def _():
        spread(w_ref[...], by_column, kron_ref)

    store_mix(kron_ref, cells_ref, out_ref)


def local_branch(features, weight, by_column):
    channels, rows, ny, nz = features.shape
    cells = pl.BlockSpec((channels, 2, ny, nz), lambda x: (0, x, 0, 0))
    return pl.pallas_call(
        functools.partial(local_kernel, by_column),
        grid=(rows // 2,),
        in_specs=[cells, whole(weight.shape)],
        out_specs=cells,
        out_shape=jax.ShapeDtypeStruct(features.shape, BF16),
        scratch_shapes=[pltpu.VMEM((channels * YB, channels * YB), BF16)],
        compiler_params=params(53),
        cost_estimate=pl.CostEstimate(flops=2 * features.size * channels, bytes_accessed=4 * features.size, transcendentals=0),
        name="local_branch",
    )(features, weight)


ROOT = math.sqrt(2.0 / math.pi)
CUBE = 0.044715 * ROOT


def gelu_slope(u):
    square = u * u
    t = jnp.tanh(u * (ROOT + CUBE * square))
    inner = u * (0.5 * ROOT + 1.5 * CUBE * square)
    return (1.0 + t) * (0.5 + (1.0 - t) * inner)


def row_copy(src, dst, sem):
    return lambda x: pltpu.make_async_copy(src.at[:, x], dst.at[:, x], sem.at[x])


def each_row(rows, act):
    def step(x, carry):
        act(x)
        return carry

    lax.fori_loop(0, rows, step, 0)


def rows_in_turn(rows, z_out_ref, b_ref, even_ref, odd_ref, arrive, use, leave):
    groups = b_ref.shape[1]

    def synthesise_z(x, g, space_ref):
        space_ref[g] = dot(b_ref[x, g], z_out_ref[...])

    for g in range(groups):
        synthesise_z(0, g, even_ref)

    def pair(i, carry):
        for n, here, there in ((0, even_ref, odd_ref), (1, odd_ref, even_ref)):
            x = 2 * i + n
            arrive(x)
            for g in range(groups):
                synthesise_z(jnp.minimum(x + 1, rows - 1), g, there)
                use(x, g, here)
            leave(x)
        return carry

    return pair


def slope_kernel(
    bias_ref, lines_ref, local_hbm, cot_hbm, y_in_ref, z_in_ref, y_out_ref, z_out_ref, grad_hbm, out_ref,
    local_ref, cot_ref, grad_ref, low_ref, b_ref, even_ref, odd_ref, g_ref, local_sem, cot_sem, grad_sem,
):
    channels, rows, ny, nz = local_ref.shape
    local_copy = row_copy(local_hbm, local_ref, local_sem)
    cot_copy = row_copy(cot_hbm, cot_ref, cot_sem)
    grad_copy = row_copy(grad_ref, grad_hbm, grad_sem)

    def begin(x):
        local_copy(x).start()
        cot_copy(x).start()

    each_row(2, begin)
    synthesise_y(lines_ref, bias_ref[...], y_out_ref, low_ref, b_ref)

    def arrive(x):
        local_copy(x).wait()
        cot_copy(x).wait()

        @pl.when(x + 2 < rows)
        def _():
            begin(x + 2)

    def use(x, g, space_ref):
        for c in range(CB):
            o = g * CB + c
            for y in range(0, ny, YB):
                at = slice(y, y + YB)
                u = space_ref[g, at, c * nz : (c + 1) * nz] + local_ref[o, x, at, :].astype(F32)
                grad_ref[o, x, at, :] = (gelu_slope(u) * cot_ref[o, x, at, :].astype(F32)).astype(BF16)

    pair = rows_in_turn(rows, z_out_ref, b_ref, even_ref, odd_ref, arrive, use, lambda x: grad_copy(x).start())

    def block(h):
        lax.fori_loop(h * XB // 2, (h + 1) * XB // 2, pair, 0)
        analyse_y(
            lambda c: grad_ref[c, pl.ds(h * XB, XB)].reshape(XB * ny, nz), 0, channels, y_in_ref[...], g_ref
        )
        total = analyse_z(z_in_ref, g_ref)
        put_lines(out_ref, h, 0, total)

    each_row(rows // XB, block)
    each_row(rows, lambda x: grad_copy(x).wait())


def space_scratch(rows, channels, ny, nz):
    groups = channels // CB
    return [
        pltpu.VMEM((2 * KY * 2 * XB, KZ * channels), BF16),
        pltpu.VMEM((rows, groups, ny, 2 * KZ * CB), BF16),
        pltpu.VMEM((groups, ny, CB * nz), F32),
        pltpu.VMEM((groups, ny, CB * nz), F32),
    ]


def slope(lines, local, cotangent, biases):
    channels, rows, ny, nz = local.shape
    y_in, z_in, y_out, z_out = plane_tables(ny, nz)
    lanes = KZ * channels
    bias_lanes = jnp.where(jnp.arange(KZ)[None, :, None] == 0, biases.reshape(-1, 1, CB), 0.0).reshape(1, lanes)
    return pl.pallas_call(
        slope_kernel,
        in_specs=[in_vmem(), in_vmem(), in_hbm(), in_hbm()] + [in_vmem()] * 4,
        out_specs=[in_hbm(), in_vmem()],
        out_shape=[
            jax.ShapeDtypeStruct(local.shape, BF16),
            jax.ShapeDtypeStruct((KY, rows // XB, 2 * XB, lanes), F32),
        ],
        scratch_shapes=[pltpu.VMEM(local.shape, BF16)] * 3
        + space_scratch(rows, channels, ny, nz)
        + [pltpu.VMEM((channels // CB * KY * 2 * XB, CB * 2 * nz), BF16)]
        + [pltpu.SemaphoreType.DMA((rows,))] * 3,
        compiler_params=params(44),
        name="slope",
    )(bias_lanes, lines, local, cotangent, jnp.asarray(y_in), jnp.asarray(z_in), jnp.asarray(y_out), jnp.asarray(z_out))


def back_kernel(
    lines_ref, local_hbm, y_out_ref, z_out_ref, out_hbm,
    local_ref, out_ref, low_ref, b_ref, even_ref, odd_ref, local_sem, out_sem,
):
    channels, rows, ny, nz = local_ref.shape
    local_copy = row_copy(local_hbm, local_ref, local_sem)
    out_copy = row_copy(out_ref, out_hbm, out_sem)
    each_row(3, lambda x: local_copy(x).start())
    synthesise_y(lines_ref, None, y_out_ref, low_ref, b_ref)

    def arrive(x):
        local_copy(x).wait()

        @pl.when(x + 3 < rows)
        def _():
            local_copy(x + 3).start()

    def use(x, g, space_ref):
        for c in range(CB):
            o = g * CB + c
            for y in range(0, ny, YB):
                at = slice(y, y + YB)
                u = space_ref[g, at, c * nz : (c + 1) * nz] + local_ref[o, x, at, :].astype(F32)
                out_ref[o, x, at, :] = u.astype(BF16)

    pair = rows_in_turn(rows, z_out_ref, b_ref, even_ref, odd_ref, arrive, use, lambda x: out_copy(x).start())
    lax.fori_loop(0, rows // 2, pair, 0)
    each_row(rows, lambda x: out_copy(x).wait())


def back(lines, local):
    channels, rows, ny, nz = local.shape
    _, _, y_out, z_out = plane_tables(ny, nz)
    return pl.pallas_call(
        back_kernel,
        in_specs=[in_vmem(), in_hbm(), in_vmem(), in_vmem()],
        out_specs=in_hbm(),
        out_shape=jax.ShapeDtypeStruct(local.shape, BF16),
        scratch_shapes=[pltpu.VMEM(local.shape, BF16)] * 2
        + space_scratch(rows, channels, ny, nz)
        + [pltpu.SemaphoreType.DMA((rows,))] * 2,
        compiler_params=params(53),
        name="back",
    )(lines, local, jnp.asarray(y_out), jnp.asarray(z_out))


def cell_sums_kernel(grad_ref, f_ref, dlines_ref, sums_ref, acc_ref):
    step = pl.program_id(0)
    channels, rows, ny, nz = f_ref.shape
    lanes = KZ * CB

    @pl.when(step == 0)
    def _():
        acc_ref[...] = jnp.zeros_like(acc_ref)

    def tiles(ref):
        return jnp.concatenate(
            [ref[:, x, y : y + YB, :].reshape(-1, nz) for x in range(rows) for y in range(0, ny, YB)], axis=1
        )

    acc_ref[...] += lax.dot_general(tiles(grad_ref), tiles(f_ref), (((1,), (1,)), ((), ())), preferred_element_type=F32)

    @pl.when(step == pl.num_programs(0) - 1)
    def _():
        n = channels * YB
        same = lax.rem(lax.broadcasted_iota(jnp.int32, (n, n), 0), YB) == lax.rem(
            lax.broadcasted_iota(jnp.int32, (n, n), 1), YB
        )
        picked = jnp.where(same, acc_ref[...], 0.0)
        fold = (
            lax.broadcasted_iota(jnp.int32, (channels, n), 1) // YB
            == lax.broadcasted_iota(jnp.int32, (channels, n), 0)
        ).astype(F32)
        half = exact_dot(fold, picked, ((1,), (0,)))
        mixing = exact_dot(half, fold, ((1,), (1,)))
        zero = dlines_ref[KY // 2].reshape(-1, KZ * channels)
        real = lax.rem(lax.broadcasted_iota(jnp.int32, (zero.shape[0], 1), 0), 2 * XB) < XB
        line = jnp.sum(jnp.where(real, zero, 0.0), axis=0, keepdims=True)
        lane = lax.broadcasted_iota(jnp.int32, (channels, KZ * channels), 1)
        channel = lax.broadcasted_iota(jnp.int32, (channels, KZ * channels), 0)
        pick = (lane == channel // CB * lanes + lax.rem(channel, CB)).astype(F32)
        biases = exact_dot(jnp.broadcast_to(line, (8, line.shape[1])), pick, ((1,), (1,)))
        packed = jnp.concatenate(
            [
                jnp.concatenate([mixing[r : r + 8] for r in range(0, channels, 8)], axis=1),
                jnp.concatenate([biases] * (channels // 8), axis=1),
            ],
            axis=0,
        )
        sums_ref[...] = jnp.broadcast_to(packed[None], sums_ref.shape)


def cell_sums(pre_grad, features, dlines, devices):
    channels, rows, ny, nz = features.shape
    cells = pl.BlockSpec((channels, 2, ny, nz), lambda x: (0, x, 0, 0))
    tile = channels * YB
    return pl.pallas_call(
        cell_sums_kernel,
        grid=(rows // 2,),
        in_specs=[cells, cells, whole(dlines.shape)],
        out_specs=whole((devices, 16, channels * channels // 8)),
        out_shape=jax.ShapeDtypeStruct((devices, 16, channels * channels // 8), F32),
        scratch_shapes=[pltpu.VMEM((tile, tile), F32)],
        compiler_params=params(53),
        name="cell_sums",
    )(pre_grad, features, dlines)


def swap(blocks):
    return lax.all_to_all(blocks, "mp", 0, 0, tiled=True)


def shards(features, cotangent, spectral_weight, pointwise_weight, biases):
    channels, rows, ny, nz = features.shape
    devices = lax.axis_size("mp")
    nx = rows * devices
    pairs = spectral_weight.shape[0]
    groups = channels // CB
    blocks = rows // XB
    cut = KZ // pairs
    cells = nx * ny * nz
    x_in, x_out = (jnp.asarray(t) for t in line_tables(nx))
    perm = jnp.asarray(lane_tables(pairs, channels))
    perm_back = jnp.asarray(lane_tables(pairs, channels).T)
    if cut == 1:
        first_k = 0
    else:
        first_k = lax.rem(lax.axis_index("mp"), cut) * pairs
    ks = jnp.broadcast_to(jnp.arange(pairs)[None, :, None] + first_k, (groups, pairs, CB)).reshape(1, -1)
    scale = jnp.where(ks == 0, 1.0, 2.0).astype(F32) / float(cells)

    def to_owner(lines):
        if cut > 1:
            lines = lines.reshape(KY, blocks, 2 * XB, groups, cut, pairs * CB)
            lines = lines.transpose(0, 4, 1, 2, 3, 5)
        return swap(lines.reshape(devices, blocks, 2 * XB, -1))

    def to_cells(lines):
        lines = swap(lines.reshape(devices, blocks, 2 * XB, -1))
        if cut > 1:
            lines = lines.reshape(KY, cut, blocks, 2 * XB, groups, pairs * CB)
            lines = lines.transpose(0, 2, 3, 4, 1, 5)
        return lines.reshape(KY, blocks, 2 * XB, -1)

    lines = to_owner(feature_lines(features))
    mixed, spec = mix_modes(lines, spectral_weight, scale, x_in, x_out, perm)
    pre_grad, dlines = slope(to_cells(mixed), local_branch(features, pointwise_weight, False), cotangent, biases)
    sums = cell_sums(pre_grad, features, dlines, devices)
    dlines, _ = lax.optimization_barrier((to_owner(dlines), sums))
    dmixed, dspec = adjoint_modes(dlines, spectral_weight, scale, x_in, x_out, perm_back)
    back_lines = to_cells(dmixed)
    spectral_grad = mode_gradient(spec, dspec)
    late_grad, _ = lax.optimization_barrier((pre_grad, dspec))
    local_back = local_branch(late_grad, pointwise_weight, True)
    total = jnp.sum(swap(sums), axis=0) * float(cells) ** -0.5
    mix_total = total[:8].reshape(8, channels // 8, channels).transpose(1, 0, 2).reshape(channels, channels)
    bias_total = total[8, :channels]
    features_grad = back(back_lines, local_back)
    return (features_grad, spectral_grad, mix_total, bias_total)


def solution(mesh):
    return jax.shard_map(
        shards,
        mesh=mesh,
        in_specs=(
            P(None, ("groups", "mp"), None, None),
            P(None, ("groups", "mp"), None, None),
            P("mp", None, None, None, None),
            P(),
            P(),
        ),
        out_specs=(
            P(None, ("groups", "mp"), None, None),
            P(("groups", "mp"), None, None, None, None),
            P("groups", None),
            P("groups"),
        ),
        check_vma=False,
    )
```

```python
import functools
import math

import jax
import jax.numpy as jnp
import ml_dtypes
import numpy as np
from jax import lax
from jax.experimental import pallas as pl
from jax.experimental.pallas import tpu as pltpu
from jax.sharding import PartitionSpec as P

KX = 16
KY = 16
KZ = 16
XB = 4
CB = 8
YB = 16
MIB = 1 << 20

F32 = jnp.float32
BF16 = jnp.bfloat16


def angles(length, modes, signed):
    freqs = np.arange(modes) - (modes // 2 if signed else 0)
    theta = (np.arange(length)[:, None] * freqs[None, :] % length) * (2.0 * math.pi / length)
    return np.cos(theta), np.sin(theta)


def bf16(table):
    return np.asarray(table, np.float32).astype(ml_dtypes.bfloat16)


@functools.cache
def plane_tables(ny, nz):
    yc, ys = angles(ny, KY, True)
    zc, zs = angles(nz, KZ, False)
    eye_x = np.eye(XB)
    rows = np.stack([np.stack([yc, -ys], 0), np.stack([-ys, -yc], 0)], 0)
    y_in = np.einsum("mryj,xw->mjrxwy", rows, eye_x).reshape(2 * KY * 2 * XB, XB * ny)
    z_in = np.einsum("mzk,cd->cmzkd", np.stack([zc, zs], 0), np.eye(CB)).reshape(CB, 2 * nz, KZ * CB)
    mix = np.stack([np.stack([yc, -ys], 0), np.stack([ys, yc], 0)], 0)
    y_out = np.einsum("qryj,xw->xqyjrw", mix, eye_x).reshape(XB, 2 * ny, KY * 2 * XB)
    z_out = np.einsum("qzk,cd->qkcdz", np.stack([zc, -zs], 0), np.eye(CB)).reshape(2 * KZ * CB, CB * nz)
    return bf16(y_in), bf16(z_in), bf16(y_out), bf16(z_out)


@functools.cache
def line_tables(nx):
    xc, xs = angles(nx, KX, True)
    inward = np.stack([np.stack([xc, -xs], 1), np.stack([xs, xc], 1)], 0)
    outward = np.stack([np.stack([xc, -xs], 1), np.stack([xs, xc], 1)], 0)
    blocks = nx // XB

    def order(table):
        return (
            table.reshape(2, blocks, XB, 2 * KX)
            .transpose(1, 0, 2, 3)
            .reshape(nx * 2, 2 * KX)
            .astype(np.float32)
        )

    return order(inward), order(outward)


def params(mib):
    return pltpu.CompilerParams(vmem_limit_bytes=mib * MIB)


def exact_dot(a, b, dims):
    return lax.dot_general(a, b, (dims, ((), ())), precision=lax.Precision.HIGHEST, preferred_element_type=F32)


def dot(a, b):
    return jnp.dot(a, b, preferred_element_type=F32)


def split3(v):
    hi = v.astype(BF16)
    rest = v - hi.astype(F32)
    mid = rest.astype(BF16)
    return hi, mid, (rest - mid.astype(F32)).astype(BF16)


def analyse_y(planes, first, count, y_in, g_ref):
    rows = y_in.shape[0] // 2
    for c in range(first, first + count, 2):
        pair = jnp.concatenate([planes(c), planes(c + 1)], axis=1)
        nz = pair.shape[1] // 2
        g = dot(y_in, pair).astype(BF16)
        for i in range(2):
            group, of_group = divmod(c + i, CB)
            for m in range(2):
                g_ref[group * rows : (group + 1) * rows, (2 * of_group + m) * nz : (2 * of_group + m + 1) * nz] = g[
                    m * rows : (m + 1) * rows, i * nz : (i + 1) * nz
                ]


def analyse_z(z_in_ref, g_ref):
    return dot(g_ref[...], z_in_ref[...].reshape(g_ref.shape[1], -1))


def put_lines(out_ref, h, first_group, total):
    rows, lanes = KY * 2 * XB, total.shape[1]
    for g in range(total.shape[0] // rows):
        first = (first_group + g) * lanes
        out_ref[:, h, :, first : first + lanes] = total[g * rows : (g + 1) * rows].reshape(KY, 2 * XB, lanes)


def in_hbm():
    return pl.BlockSpec(memory_space=pltpu.HBM)


def in_vmem():
    return pl.BlockSpec(memory_space=pltpu.VMEM)


DEPTH = 3
PER_COPY = 4
PER_DOT = 16


def lines_kernel(f_hbm, y_in_hbm, z_in_hbm, out_ref, f_ref, g_ref, y_in_ref, z_in_ref, sem, table_sem):
    channels, rows, ny, nz = f_ref.shape
    copies = [
        pltpu.make_async_copy(f_hbm.at[pl.ds(c, PER_COPY)], f_ref.at[pl.ds(c, PER_COPY)], sem.at[c // PER_COPY])
        for c in range(0, channels, PER_COPY)
    ]
    tables = [
        pltpu.make_async_copy(y_in_hbm, y_in_ref, table_sem.at[0]),
        pltpu.make_async_copy(z_in_hbm, z_in_ref, table_sem.at[1]),
    ]
    tables[0].start()
    for copy in copies[:DEPTH]:
        copy.start()
    tables[1].start()
    tables[0].wait()
    y_in = y_in_ref[...]
    for first in range(0, channels, PER_DOT):
        for c in range(0, PER_DOT, PER_COPY):
            n = (first + c) // PER_COPY
            copies[n].wait()
            if n + DEPTH < len(copies):
                copies[n + DEPTH].start()
            for h in range(rows // XB):
                analyse_y(
                    lambda i: f_ref[first + i, h * XB : (h + 1) * XB].reshape(XB * ny, nz), c, PER_COPY, y_in, g_ref.at[h]
                )
        if first == 0:
            tables[1].wait()
        for h in range(rows // XB):
            put_lines(out_ref, h, first // CB, analyse_z(z_in_ref, g_ref.at[h]))


def feature_lines(features):
    channels, rows, ny, nz = features.shape
    y_in, z_in, _, _ = plane_tables(ny, nz)
    blocks = rows // XB
    return pl.pallas_call(
        lines_kernel,
        in_specs=[in_hbm()] * 3,
        out_specs=in_vmem(),
        out_shape=jax.ShapeDtypeStruct((KY, blocks, 2 * XB, KZ * channels), F32),
        scratch_shapes=[
            pltpu.VMEM(features.shape, BF16),
            pltpu.VMEM((blocks, PER_DOT // CB * KY * 2 * XB, CB * 2 * nz), BF16),
            pltpu.VMEM(y_in.shape, BF16),
            pltpu.VMEM(z_in.shape, BF16),
            pltpu.SemaphoreType.DMA((channels // PER_COPY,)),
            pltpu.SemaphoreType.DMA((2,)),
        ],
        compiler_params=params(60),
        name="feature_lines",
    )(features, jnp.asarray(y_in), jnp.asarray(z_in))


def quad_of(channels):
    return 128 // channels


def chosen(shape, rule):
    row = lax.broadcasted_iota(jnp.int32, (shape[0], 1), 0)
    column = lax.broadcasted_iota(jnp.int32, (1, shape[1]), 1)
    return jnp.where(rule(row, column), 1.0, 0.0).astype(BF16)


def lane_order(lane, pairs, channels):
    per_group = pairs * CB
    return lax.rem(lane, per_group) // CB * channels + lane // per_group * CB + lax.rem(lane, CB)


def quad_columns(table, channels):
    quad = quad_of(channels)
    return table.reshape(-1, 2, KX // quad, quad).transpose(0, 3, 1, 2).reshape(table.shape)


def pack_kernel(w_ref, out_ref):
    pairs, _, kx, channels, _ = w_ref.shape
    quad = quad_of(channels)
    for k in range(pairs):
        for part in range(2):
            for t in range(kx // quad):
                out_ref[k, part, t] = jnp.concatenate([w_ref[k, part, t * quad + q] for q in range(quad)], axis=1)


def pack_weights(weight):
    pairs, _, kx, channels, _ = weight.shape
    quad = quad_of(channels)
    shape = (pairs, 2, kx // quad, channels, quad * channels)
    return pl.pallas_call(
        pack_kernel,
        grid=(pairs // PER_STEP,),
        in_specs=[pl.BlockSpec((PER_STEP,) + weight.shape[1:], lambda k: (k, 0, 0, 0, 0))],
        out_specs=pl.BlockSpec((PER_STEP,) + shape[1:], lambda k: (k, 0, 0, 0, 0)),
        out_shape=jax.ShapeDtypeStruct(shape, F32),
        compiler_params=params(53),
        cost_estimate=pl.CostEstimate(flops=0, bytes_accessed=8 * weight.size * quad, transcendentals=0),
        name="pack_weights",
    )(weight)


def columns(spec_ref, k, pairs, channels):
    groups = channels // CB
    per_group = pairs * CB
    return jnp.concatenate(
        [spec_ref[pl.ds(pl.multiple_of(g * per_group + k * CB, CB), CB), :] for g in range(groups)], axis=0
    )


def mix_kernel(
    scale_ref, lines_ref, w_hbm, x_in_ref, x_out_ref, out_ref, spec_ref, w_ref, wide_ref, rows_ref, sem
):
    pairs, _, turns, channels, lanes = w_ref.shape
    copy = pltpu.make_async_copy(w_hbm, w_ref, sem)
    copy.start()
    spec = exact_dot(lines_ref[...].reshape(x_in_ref.shape[0], -1).T, x_in_ref[...], ((1,), (0,)))
    spec_ref[...] = spec
    over = chosen((6 * KX, 2 * KX * channels), lambda row, lane: lax.rem(row, 2 * KX) == lane // channels)
    wide_ref[...] = dot(jnp.concatenate(split3(spec), axis=1), over)
    copy.wait()

    def step(k, carry):
        v = columns(wide_ref, k, pairs, channels)
        reals, imags = [], []
        for t in range(turns):
            vr, vi = v[:, t * lanes : (t + 1) * lanes], v[:, (turns + t) * lanes : (turns + t + 1) * lanes]
            wr, wi = w_ref[k, 0, t], w_ref[k, 1, t]
            reals.append(jnp.sum(vr * wr - vi * wi, axis=0, keepdims=True))
            imags.append(jnp.sum(vr * wi + vi * wr, axis=0, keepdims=True))
        rows_ref[k] = jnp.concatenate(reals + imags, axis=0)
        return carry

    lax.fori_loop(0, pairs, step, 0, unroll=2)
    mixed = jnp.concatenate(
        [
            jnp.concatenate([rows_ref[k, :, q * channels : (q + 1) * channels] for k in range(pairs)], axis=1)
            for q in range(lanes // channels)
        ],
        axis=0,
    )
    order = chosen((mixed.shape[1],) * 2, lambda row, lane: row == lane_order(lane, pairs, channels))
    parts = dot(jnp.concatenate(split3(mixed), axis=0), order)
    n = mixed.shape[0]
    placed = (parts[2 * n :] + parts[n : 2 * n]) + parts[:n]
    out_ref[...] = exact_dot(x_out_ref[...], placed * scale_ref[...], ((1,), (0,))).reshape(out_ref.shape)


def whole(shape):
    return pl.BlockSpec(shape, lambda k: (0,) * len(shape))


def mix_modes(lines, packed, scale, x_in, x_out):
    pairs, _, turns, channels, wide = packed.shape
    lanes = pairs * channels
    return pl.pallas_call(
        mix_kernel,
        in_specs=[in_vmem(), in_vmem(), in_hbm()] + [in_vmem()] * 2,
        out_specs=[in_vmem(), in_vmem()],
        out_shape=[jax.ShapeDtypeStruct(lines.shape, F32), jax.ShapeDtypeStruct((lanes, 2 * KX), F32)],
        scratch_shapes=[
            pltpu.VMEM(packed.shape, F32),
            pltpu.VMEM((lanes, 2 * turns * wide), F32),
            pltpu.VMEM((pairs, 2 * turns, wide), F32),
            pltpu.SemaphoreType.DMA,
        ],
        compiler_params=params(53),
        name="mix_modes",
    )(scale, lines, packed, jnp.asarray(x_in), jnp.asarray(quad_columns(x_out, channels)))


def adjoint_kernel(
    scale_ref, lines_ref, w_hbm, x_in_ref, x_out_ref, sums_ref, out_ref, dspec_ref,
    w_ref, rows_ref, prod_ref, sem,
):
    pairs, _, turns, channels, lanes = w_ref.shape
    copy = pltpu.make_async_copy(w_hbm, w_ref, sem)
    copy.start()
    placed = exact_dot(x_in_ref[...].T, lines_ref[...].reshape(x_in_ref.shape[0], -1), ((1,), (0,))) * scale_ref[...]
    n = placed.shape[0]
    order = chosen((placed.shape[1],) * 2, lambda row, lane: lane_order(row, pairs, channels) == lane)
    parts = dot(jnp.concatenate(split3(placed), axis=0), order)
    rows = (parts[2 * n :] + parts[n : 2 * n]) + parts[:n]
    per = 2 * turns
    for k in range(pairs):
        mine = rows[:, k * channels : (k + 1) * channels]
        dspec_ref[k] = mine
        rows_ref[k] = jnp.concatenate([mine[q * per : (q + 1) * per] for q in range(lanes // channels)], axis=1)
    copy.wait()
    half = per * lanes

    def step(k, carry):
        d = rows_ref[k]
        at = pl.ds(pl.multiple_of(k * channels, channels), channels)
        for t in range(turns):
            dr, di = d[t : t + 1], d[turns + t : turns + t + 1]
            wr, wi = w_ref[k, 0, t], w_ref[k, 1, t]
            for part, value in enumerate((dr * wr + di * wi, di * wr - dr * wi)):
                first = (part * turns + t) * lanes
                hi = value.astype(BF16)
                prod_ref[at, first : first + lanes] = hi
                prod_ref[at, half + first : half + first + lanes] = (value - hi.astype(F32)).astype(BF16)
        return carry

    lax.fori_loop(0, pairs, step, 0, unroll=2)
    fold = chosen(
        (2 * half, 2 * KX),
        lambda row, lane: lax.rem(row, half) // channels == lax.rem(lane, per) * (lanes // channels) + lane // per,
    )
    sums = dot(prod_ref[...], fold)
    cols = jnp.concatenate(
        [
            sums[k * channels + g * CB : k * channels + (g + 1) * CB]
            for g in range(channels // CB)
            for k in range(pairs)
        ],
        axis=0,
    )
    lines = exact_dot(x_out_ref[...], cols, ((1,), (1,)))
    out_ref[:, :, :, : lines.shape[1]] = lines.reshape(lines_ref.shape)
    out_ref[:, :, :, lines.shape[1] :] = jnp.broadcast_to(sums_ref[...][None], out_ref.shape[:1] + sums_ref.shape)


def adjoint_modes(lines, packed, scale, x_in, x_out, sums):
    pairs, _, turns, channels, wide = packed.shape
    return pl.pallas_call(
        adjoint_kernel,
        in_specs=[in_vmem(), in_vmem(), in_hbm()] + [in_vmem()] * 3,
        out_specs=[in_vmem(), in_vmem()],
        out_shape=[
            jax.ShapeDtypeStruct(lines.shape[:3] + (lines.shape[3] + sums.shape[2],), F32),
            jax.ShapeDtypeStruct((pairs, 2 * KX, channels), F32),
        ],
        scratch_shapes=[
            pltpu.VMEM(packed.shape, F32),
            pltpu.VMEM((pairs, 2 * turns, wide), F32),
            pltpu.VMEM((pairs * channels, 4 * turns * wide), BF16),
            pltpu.SemaphoreType.DMA,
        ],
        compiler_params=params(53),
        name="adjoint_modes",
    )(
        scale,
        lines,
        packed,
        jnp.asarray(quad_columns(x_in, channels)),
        jnp.asarray(quad_columns(x_out, channels)),
        sums,
    )


PER_STEP = 4


def outer_kernel(spec_ref, dspec_ref, out_ref):
    channels = dspec_ref.shape[-1]
    pairs = spec_ref.shape[0] // channels
    quad = quad_of(channels)
    per = 2 * KX // quad
    for i in range(PER_STEP):
        v = columns(spec_ref, pl.program_id(0) * PER_STEP + i, pairs, channels)
        d = dspec_ref[i]
        for a in range(KX):
            vr, vi = v[:, a : a + 1], v[:, KX + a : KX + a + 1]
            t, q = divmod(a, quad)
            dr = d[q * per + t : q * per + t + 1]
            di = d[q * per + per // 2 + t : q * per + per // 2 + t + 1]
            out_ref[i, 0, a] = vr * dr + vi * di
            out_ref[i, 1, a] = vr * di - vi * dr


def mode_gradient(spec, dspec):
    pairs, twice_kx, channels = dspec.shape
    shape = (pairs, 2, twice_kx // 2, channels, channels)
    return pl.pallas_call(
        outer_kernel,
        grid=(pairs // PER_STEP,),
        in_specs=[whole(spec.shape), pl.BlockSpec((PER_STEP, twice_kx, channels), lambda k: (k, 0, 0))],
        out_specs=pl.BlockSpec((PER_STEP,) + shape[1:], lambda k: (k, 0, 0, 0, 0)),
        out_shape=jax.ShapeDtypeStruct(shape, F32),
        compiler_params=params(24),
        name="mode_gradient",
    )(spec, dspec)


def spread(w, by_column, out_ref):
    n = out_ref.shape[0]
    fold = (
        lax.broadcasted_iota(jnp.int32, (n, w.shape[0]), 0) // YB
        == lax.broadcasted_iota(jnp.int32, (n, w.shape[0]), 1)
    ).astype(F32).astype(BF16)
    wide = lax.dot_general(fold, w, (((1,), (1 if by_column else 0,)), ((), ())), preferred_element_type=F32)
    full = lax.dot_general(wide.astype(BF16), fold, (((1,), (1,)), ((), ())), preferred_element_type=F32)
    same = lax.rem(lax.broadcasted_iota(jnp.int32, (n, n), 0), YB) == lax.rem(
        lax.broadcasted_iota(jnp.int32, (n, n), 1), YB
    )
    out_ref[...] = jnp.where(same, full, 0.0).astype(BF16)


def synthesise_y(lines_ref, bias, y_out_ref, low_ref, b_ref):
    rows = KY * 2 * XB
    lanes = KZ * CB
    ny = b_ref.shape[2]
    tables = y_out_ref[...].reshape(-1, rows)
    tables = jnp.concatenate([tables, tables], axis=1)
    for h in range(lines_ref.shape[1]):
        block = lines_ref[:, h, :, : low_ref.shape[1]].reshape(rows, low_ref.shape[1])
        if bias is not None:
            row = lax.broadcasted_iota(jnp.int32, (rows, 1), 0) // XB
            block = block + jnp.where(row == KY // 2 * 2, bias, 0.0)
        hi = block.astype(BF16)
        low_ref[:rows] = hi
        low_ref[rows:] = (block - hi.astype(F32)).astype(BF16)
        b = dot(tables, low_ref[...]).astype(BF16)
        for x in range(XB):
            for part in range(2):
                first = (2 * x + part) * ny
                for g in range(b_ref.shape[1]):
                    b_ref[h * XB + x, g, :, part * lanes : (part + 1) * lanes] = b[
                        first : first + ny, g * lanes : (g + 1) * lanes
                    ]


def channel_mix(kron, cells_ref, x, y):
    nz = cells_ref.shape[-1]
    tiles = [cells_ref[:, x, y + t * YB : y + (t + 1) * YB, :].reshape(-1, nz) for t in range(2)]
    return dot(kron, jnp.concatenate(tiles, axis=1))


def store_mix(kron_ref, cells_ref, out_ref):
    channels, rows, ny, nz = cells_ref.shape
    for x in range(rows):
        for y in range(0, ny, 2 * YB):
            local = channel_mix(kron_ref[...], cells_ref, x, y).astype(BF16)
            for t in range(2):
                out_ref[:, x, y + t * YB : y + (t + 1) * YB, :] = local[:, t * nz : (t + 1) * nz].reshape(
                    channels, YB, nz
                )


def local_kernel(by_column, cells_ref, w_ref, out_ref, kron_ref):
    @pl.when(pl.program_id(0) == 0)
    def _():
        spread(w_ref[...], by_column, kron_ref)

    store_mix(kron_ref, cells_ref, out_ref)


def local_branch(features, weight, by_column):
    channels, rows, ny, nz = features.shape
    cells = pl.BlockSpec((channels, 2, ny, nz), lambda x: (0, x, 0, 0))
    return pl.pallas_call(
        functools.partial(local_kernel, by_column),
        grid=(rows // 2,),
        in_specs=[cells, whole(weight.shape)],
        out_specs=cells,
        out_shape=jax.ShapeDtypeStruct(features.shape, BF16),
        scratch_shapes=[pltpu.VMEM((channels * YB, channels * YB), BF16)],
        compiler_params=params(53),
        cost_estimate=pl.CostEstimate(flops=2 * features.size * channels, bytes_accessed=4 * features.size, transcendentals=0),
        name="local_branch",
    )(features, weight)


ROOT = math.sqrt(2.0 / math.pi)
CUBE = 0.044715 * ROOT


def gelu_slope(u):
    square = u * u
    t = jnp.tanh(u * (ROOT + CUBE * square))
    inner = u * (0.5 * ROOT + 1.5 * CUBE * square)
    return (1.0 + t) * (0.5 + (1.0 - t) * inner)


def row_copy(src, dst, sem):
    return lambda x: pltpu.make_async_copy(src.at[:, x], dst.at[:, x], sem.at[x])


def each_row(rows, act):
    def step(x, carry):
        act(x)
        return carry

    lax.fori_loop(0, rows, step, 0)


def rows_in_turn(rows, z_out_ref, b_ref, even_ref, odd_ref, arrive, use, leave):
    groups = b_ref.shape[1]

    lanes = even_ref.shape[2] // CB * PER_USE

    def synthesise_z(x, g, c, space_ref):
        at = slice(c // PER_USE * lanes, (c // PER_USE + 1) * lanes)
        space_ref[g, :, at] = dot(b_ref[x, g], z_out_ref[:, at])

    for g in range(groups):
        for c in range(0, CB, PER_USE):
            synthesise_z(0, g, c, even_ref)

    def pair(i, carry):
        for n, here, there in ((0, even_ref, odd_ref), (1, odd_ref, even_ref)):
            x = 2 * i + n
            arrive(x)
            for g in range(groups):
                for c in range(0, CB, PER_USE):
                    synthesise_z(jnp.minimum(x + 1, rows - 1), g, c, there)
                    use(x, g, c, here)
            leave(x)
        return carry

    return pair


PER_USE = 8


def slope_kernel(
    bias_ref, lines_ref, local_hbm, cot_hbm, y_in_ref, z_in_ref, y_out_ref, z_out_ref, grad_hbm, out_ref,
    local_ref, cot_ref, grad_ref, low_ref, b_ref, even_ref, odd_ref, g_ref, local_sem, cot_sem, grad_sem,
):
    channels, rows, ny, nz = local_ref.shape
    local_copy = row_copy(local_hbm, local_ref, local_sem)
    cot_copy = row_copy(cot_hbm, cot_ref, cot_sem)
    grad_copy = row_copy(grad_ref, grad_hbm, grad_sem)

    def begin(x):
        local_copy(x).start()
        cot_copy(x).start()

    each_row(2, begin)
    synthesise_y(lines_ref, bias_ref[...], y_out_ref, low_ref, b_ref)

    def arrive(x):
        local_copy(x).wait()
        cot_copy(x).wait()

        @pl.when(x + 2 < rows)
        def _():
            begin(x + 2)

    def use(x, g, first, space_ref):
        for c in range(first, first + PER_USE):
            o = g * CB + c
            for y in range(0, ny, YB):
                at = slice(y, y + YB)
                u = space_ref[g, at, c * nz : (c + 1) * nz] + local_ref[o, x, at, :].astype(F32)
                grad_ref[o, x, at, :] = (gelu_slope(u) * cot_ref[o, x, at, :].astype(F32)).astype(BF16)

    pair = rows_in_turn(rows, z_out_ref, b_ref, even_ref, odd_ref, arrive, use, lambda x: grad_copy(x).start())

    def block(h):
        lax.fori_loop(h * XB // 2, (h + 1) * XB // 2, pair, 0)
        analyse_y(
            lambda c: grad_ref[c, pl.ds(h * XB, XB)].reshape(XB * ny, nz), 0, channels, y_in_ref[...], g_ref
        )
        total = analyse_z(z_in_ref, g_ref)
        put_lines(out_ref, h, 0, total)

    each_row(rows // XB, block)
    each_row(rows, lambda x: grad_copy(x).wait())


def space_scratch(rows, channels, ny, nz):
    groups = channels // CB
    return [
        pltpu.VMEM((2 * KY * 2 * XB, KZ * channels), BF16),
        pltpu.VMEM((rows, groups, ny, 2 * KZ * CB), BF16),
        pltpu.VMEM((groups, ny, CB * nz), F32),
        pltpu.VMEM((groups, ny, CB * nz), F32),
    ]


def slope(lines, local, cotangent, biases):
    channels, rows, ny, nz = local.shape
    y_in, z_in, y_out, z_out = plane_tables(ny, nz)
    lanes = KZ * channels
    bias_lanes = jnp.where(jnp.arange(KZ)[None, :, None] == 0, biases.reshape(-1, 1, CB), 0.0).reshape(1, lanes)
    return pl.pallas_call(
        slope_kernel,
        in_specs=[in_vmem(), in_vmem(), in_hbm(), in_hbm()] + [in_vmem()] * 4,
        out_specs=[in_hbm(), in_vmem()],
        out_shape=[
            jax.ShapeDtypeStruct(local.shape, BF16),
            jax.ShapeDtypeStruct((KY, rows // XB, 2 * XB, lanes), F32),
        ],
        scratch_shapes=[pltpu.VMEM(local.shape, BF16)] * 3
        + space_scratch(rows, channels, ny, nz)
        + [pltpu.VMEM((channels // CB * KY * 2 * XB, CB * 2 * nz), BF16)]
        + [pltpu.SemaphoreType.DMA((rows,))] * 3,
        compiler_params=params(44),
        name="slope",
    )(bias_lanes, lines, local, cotangent, jnp.asarray(y_in), jnp.asarray(z_in), jnp.asarray(y_out), jnp.asarray(z_out))


def back_kernel(
    factor, lines_ref, sums_ref, local_hbm, y_out_ref, z_out_ref, out_hbm, mix_ref, bias_ref,
    local_ref, out_ref, low_ref, b_ref, even_ref, odd_ref, local_sem, out_sem,
):
    channels, rows, ny, nz = local_ref.shape
    local_copy = row_copy(local_hbm, local_ref, local_sem)
    out_copy = row_copy(out_ref, out_hbm, out_sem)
    each_row(3, lambda x: local_copy(x).start())
    synthesise_y(lines_ref, None, y_out_ref, low_ref, b_ref)
    wide = channels * channels // 8
    total = jnp.sum(sums_ref[...], axis=0) * factor
    mixing, biases = total[0, :, :wide], total[-1, :, total.shape[2] - wide :]
    mix_ref[...] = jnp.concatenate([mixing[:, c : c + channels] for c in range(0, wide, channels)], axis=0)
    bias_ref[...] = biases[:1, :channels]

    def arrive(x):
        local_copy(x).wait()

        @pl.when(x + 3 < rows)
        def _():
            local_copy(x + 3).start()

    def use(x, g, first, space_ref):
        for c in range(first, first + PER_USE):
            o = g * CB + c
            for y in range(0, ny, YB):
                at = slice(y, y + YB)
                u = space_ref[g, at, c * nz : (c + 1) * nz] + local_ref[o, x, at, :].astype(F32)
                out_ref[o, x, at, :] = u.astype(BF16)

    pair = rows_in_turn(rows, z_out_ref, b_ref, even_ref, odd_ref, arrive, use, lambda x: out_copy(x).start())
    lax.fori_loop(0, rows // 2, pair, 0)
    each_row(rows, lambda x: out_copy(x).wait())


def back(lines, sums, local, factor):
    channels, rows, ny, nz = local.shape
    _, _, y_out, z_out = plane_tables(ny, nz)
    return pl.pallas_call(
        functools.partial(back_kernel, factor),
        in_specs=[in_vmem(), in_vmem(), in_hbm(), in_vmem(), in_vmem()],
        out_specs=[in_hbm(), in_vmem(), in_vmem()],
        out_shape=[
            jax.ShapeDtypeStruct(local.shape, BF16),
            jax.ShapeDtypeStruct((channels, channels), F32),
            jax.ShapeDtypeStruct((1, channels), F32),
        ],
        scratch_shapes=[pltpu.VMEM(local.shape, BF16)] * 2
        + space_scratch(rows, channels, ny, nz)
        + [pltpu.SemaphoreType.DMA((rows,))] * 2,
        compiler_params=params(53),
        name="back",
    )(lines, sums, local, jnp.asarray(y_out), jnp.asarray(z_out))


def cell_sums_kernel(grad_ref, f_ref, dlines_ref, sums_ref, acc_ref):
    step = pl.program_id(0)
    channels, rows, ny, nz = f_ref.shape
    lanes = KZ * CB

    @pl.when(step == 0)
    def _():
        acc_ref[...] = jnp.zeros_like(acc_ref)

    def tiles(ref):
        return jnp.concatenate(
            [ref[:, x, y : y + YB, :].reshape(-1, nz) for x in range(rows) for y in range(0, ny, YB)], axis=1
        )

    acc_ref[...] += lax.dot_general(tiles(grad_ref), tiles(f_ref), (((1,), (1,)), ((), ())), preferred_element_type=F32)

    @pl.when(step == pl.num_programs(0) - 1)
    def _():
        n = channels * YB
        same = lax.rem(lax.broadcasted_iota(jnp.int32, (n, n), 0), YB) == lax.rem(
            lax.broadcasted_iota(jnp.int32, (n, n), 1), YB
        )
        picked = jnp.where(same, acc_ref[...], 0.0)
        fold = (
            lax.broadcasted_iota(jnp.int32, (channels, n), 1) // YB
            == lax.broadcasted_iota(jnp.int32, (channels, n), 0)
        ).astype(F32)
        half = exact_dot(fold, picked, ((1,), (0,)))
        mixing = exact_dot(half, fold, ((1,), (1,)))
        zero = dlines_ref[KY // 2].reshape(-1, KZ * channels)
        real = lax.rem(lax.broadcasted_iota(jnp.int32, (zero.shape[0], 1), 0), 2 * XB) < XB
        line = jnp.sum(jnp.where(real, zero, 0.0), axis=0, keepdims=True)
        lane = lax.broadcasted_iota(jnp.int32, (channels, KZ * channels), 1)
        channel = lax.broadcasted_iota(jnp.int32, (channels, KZ * channels), 0)
        pick = (lane == channel // CB * lanes + lax.rem(channel, CB)).astype(F32)
        biases = exact_dot(jnp.broadcast_to(line, (8, line.shape[1])), pick, ((1,), (1,)))
        packed = [
            jnp.concatenate([mixing[r : r + 8] for r in range(0, channels, 8)], axis=1),
            jnp.concatenate([biases] * (channels // 8), axis=1),
        ]
        if sums_ref.shape[0] == 1:
            sums_ref[0] = jnp.concatenate(packed, axis=1)
        else:
            for h in range(sums_ref.shape[0]):
                sums_ref[h] = packed[min(h, 1)]


def cell_sums(pre_grad, features, dlines):
    channels, rows, ny, nz = features.shape
    cells = pl.BlockSpec((channels, 2, ny, nz), lambda x: (0, x, 0, 0))
    tile = channels * YB
    blocks = rows // XB
    shape = (blocks, 8, channels * channels // 8 * (2 if blocks == 1 else 1))
    return pl.pallas_call(
        cell_sums_kernel,
        grid=(rows // 2,),
        in_specs=[cells, cells, whole(dlines.shape)],
        out_specs=whole(shape),
        out_shape=jax.ShapeDtypeStruct(shape, F32),
        scratch_shapes=[pltpu.VMEM((tile, tile), F32)],
        compiler_params=params(53),
        name="cell_sums",
    )(pre_grad, features, dlines)


def swap(blocks):
    return lax.all_to_all(blocks, "mp", 0, 0, tiled=True)


def shards(features, cotangent, spectral_weight, pointwise_weight, biases):
    channels, rows, ny, nz = features.shape
    devices = lax.axis_size("mp")
    nx = rows * devices
    pairs = spectral_weight.shape[0]
    groups = channels // CB
    blocks = rows // XB
    cut = KZ // pairs
    cells = nx * ny * nz
    x_in, x_out = line_tables(nx)
    if cut == 1:
        first_k = 0
    else:
        first_k = lax.rem(lax.axis_index("mp"), cut) * pairs
    ks = jnp.broadcast_to(jnp.arange(pairs)[None, :, None] + first_k, (groups, pairs, CB)).reshape(1, -1)
    scale = jnp.where(ks == 0, 1.0, 2.0).astype(F32) / float(cells)

    def to_owner(lines):
        if cut > 1:
            lines = lines.reshape(KY, blocks, 2 * XB, groups, cut, pairs * CB)
            lines = lines.transpose(0, 4, 1, 2, 3, 5)
        return swap(lines.reshape(devices, blocks, 2 * XB, -1))

    def to_cells(lines):
        lines = swap(lines)
        own = pairs * channels
        extra = lines[..., own:]
        if cut > 1:
            lines = lines[..., :own].reshape(KY, cut, blocks, 2 * XB, groups, pairs * CB)
            lines = lines.transpose(0, 2, 3, 4, 1, 5).reshape(KY, blocks, 2 * XB, -1)
        return lines, extra

    lines = to_owner(feature_lines(features))
    packed = pack_weights(spectral_weight)
    lines, packed = lax.optimization_barrier((lines, packed))
    mixed, spec = mix_modes(lines, packed, scale, x_in, x_out)
    pre_grad, dlines = slope(to_cells(mixed)[0], local_branch(features, pointwise_weight, False), cotangent, biases)
    sums = cell_sums(pre_grad, features, dlines)
    dlines = to_owner(dlines)
    dmixed, dspec = adjoint_modes(dlines, packed, scale, x_in, x_out, sums)
    back_lines, sums = to_cells(dmixed)
    spectral_grad = mode_gradient(spec, dspec)
    late_grad, _ = lax.optimization_barrier((pre_grad, dspec))
    local_back = local_branch(late_grad, pointwise_weight, True)
    features_grad, mix_total, bias_total = back(back_lines, sums, local_back, float(cells) ** -0.5)
    return (features_grad, spectral_grad, mix_total, bias_total[0])


def solution(mesh):
    return jax.shard_map(
        shards,
        mesh=mesh,
        in_specs=(
            P(None, ("groups", "mp"), None, None),
            P(None, ("groups", "mp"), None, None),
            P("mp", None, None, None, None),
            P(),
            P(),
        ),
        out_specs=(
            P(None, ("groups", "mp"), None, None),
            P(("groups", "mp"), None, None, None, None),
            P("groups", None),
            P("groups"),
        ),
        check_vma=False,
    )
```

```python
import functools
import math

import jax
import jax.numpy as jnp
import ml_dtypes
import numpy as np
from jax import lax
from jax.experimental import pallas as pl
from jax.experimental.pallas import tpu as pltpu
from jax.sharding import PartitionSpec as P

KX = 16
KY = 16
KZ = 16
XB = 4
CB = 8
YB = 16
MIB = 1 << 20

F32 = jnp.float32
BF16 = jnp.bfloat16


def angles(length, modes, signed):
    freqs = np.arange(modes) - (modes // 2 if signed else 0)
    theta = (np.arange(length)[:, None] * freqs[None, :] % length) * (2.0 * math.pi / length)
    return np.cos(theta), np.sin(theta)


def bf16(table):
    return np.asarray(table, np.float32).astype(ml_dtypes.bfloat16)


@functools.cache
def plane_tables(ny, nz):
    yc, ys = angles(ny, KY, True)
    zc, zs = angles(nz, KZ, False)
    eye_x = np.eye(XB)
    rows = np.stack([np.stack([yc, -ys], 0), np.stack([-ys, -yc], 0)], 0)
    y_in = np.einsum("mryj,xw->mjrxwy", rows, eye_x).reshape(2 * KY * 2 * XB, XB * ny)
    z_in = np.einsum("mzk,cd->cmzkd", np.stack([zc, zs], 0), np.eye(CB)).reshape(CB, 2 * nz, KZ * CB)
    mix = np.stack([np.stack([yc, -ys], 0), np.stack([ys, yc], 0)], 0)
    y_out = np.einsum("qryj,xw->xqyjrw", mix, eye_x).reshape(XB, 2 * ny, KY * 2 * XB)
    z_out = np.einsum("qzk,cd->qkcdz", np.stack([zc, -zs], 0), np.eye(CB)).reshape(2 * KZ * CB, CB * nz)
    return bf16(y_in), bf16(z_in), bf16(y_out), bf16(z_out)


@functools.cache
def line_tables(nx):
    xc, xs = angles(nx, KX, True)
    inward = np.stack([np.stack([xc, -xs], 1), np.stack([xs, xc], 1)], 0)
    outward = np.stack([np.stack([xc, -xs], 1), np.stack([xs, xc], 1)], 0)
    blocks = nx // XB

    def order(table):
        return (
            table.reshape(2, blocks, XB, 2 * KX)
            .transpose(1, 0, 2, 3)
            .reshape(nx * 2, 2 * KX)
            .astype(np.float32)
        )

    return order(inward), order(outward)


def params(mib):
    return pltpu.CompilerParams(vmem_limit_bytes=mib * MIB)


def exact_dot(a, b, dims):
    return lax.dot_general(a, b, (dims, ((), ())), precision=lax.Precision.HIGHEST, preferred_element_type=F32)


def dot(a, b):
    return jnp.dot(a, b, preferred_element_type=F32)


def split3(v):
    hi = v.astype(BF16)
    rest = v - hi.astype(F32)
    mid = rest.astype(BF16)
    return hi, mid, (rest - mid.astype(F32)).astype(BF16)


def analyse_y(planes, first, count, y_in, g_ref):
    rows = y_in.shape[0] // 2
    for c in range(first, first + count, 2):
        pair = jnp.concatenate([planes(c), planes(c + 1)], axis=1)
        nz = pair.shape[1] // 2
        g = dot(y_in, pair).astype(BF16)
        for i in range(2):
            group, of_group = divmod(c + i, CB)
            for m in range(2):
                g_ref[group * rows : (group + 1) * rows, (2 * of_group + m) * nz : (2 * of_group + m + 1) * nz] = g[
                    m * rows : (m + 1) * rows, i * nz : (i + 1) * nz
                ]


def analyse_z(z_in_ref, g_ref):
    return dot(g_ref[...], z_in_ref[...].reshape(g_ref.shape[1], -1))


def put_lines(out_ref, h, first_group, total):
    rows, lanes = KY * 2 * XB, total.shape[1]
    for g in range(total.shape[0] // rows):
        first = (first_group + g) * lanes
        out_ref[:, h, :, first : first + lanes] = total[g * rows : (g + 1) * rows].reshape(KY, 2 * XB, lanes)


def in_hbm():
    return pl.BlockSpec(memory_space=pltpu.HBM)


def in_vmem():
    return pl.BlockSpec(memory_space=pltpu.VMEM)


DEPTH = 2
PER_COPY = 8
PER_DOT = 16


def lines_kernel(f_hbm, y_in_hbm, z_in_hbm, out_ref, f_ref, g_ref, y_in_ref, z_in_ref, sem, table_sem):
    channels, rows, ny, nz = f_ref.shape
    copies = [
        pltpu.make_async_copy(f_hbm.at[pl.ds(c, PER_COPY)], f_ref.at[pl.ds(c, PER_COPY)], sem.at[c // PER_COPY])
        for c in range(0, channels, PER_COPY)
    ]
    tables = [
        pltpu.make_async_copy(y_in_hbm, y_in_ref, table_sem.at[0]),
        pltpu.make_async_copy(z_in_hbm, z_in_ref, table_sem.at[1]),
    ]
    tables[0].start()
    for copy in copies[:DEPTH]:
        copy.start()
    tables[1].start()
    tables[0].wait()
    y_in = y_in_ref[...]
    for first in range(0, channels, PER_DOT):
        for c in range(0, PER_DOT, PER_COPY):
            n = (first + c) // PER_COPY
            copies[n].wait()
            if n + DEPTH < len(copies):
                copies[n + DEPTH].start()
            for h in range(rows // XB):
                analyse_y(
                    lambda i: f_ref[first + i, h * XB : (h + 1) * XB].reshape(XB * ny, nz), c, PER_COPY, y_in, g_ref.at[h]
                )
        if first == 0:
            tables[1].wait()
        for h in range(rows // XB):
            put_lines(out_ref, h, first // CB, analyse_z(z_in_ref, g_ref.at[h]))


def feature_lines(features):
    channels, rows, ny, nz = features.shape
    y_in, z_in, _, _ = plane_tables(ny, nz)
    blocks = rows // XB
    return pl.pallas_call(
        lines_kernel,
        in_specs=[in_hbm()] * 3,
        out_specs=in_vmem(),
        out_shape=jax.ShapeDtypeStruct((KY, blocks, 2 * XB, KZ * channels), F32),
        scratch_shapes=[
            pltpu.VMEM(features.shape, BF16),
            pltpu.VMEM((blocks, PER_DOT // CB * KY * 2 * XB, CB * 2 * nz), BF16),
            pltpu.VMEM(y_in.shape, BF16),
            pltpu.VMEM(z_in.shape, BF16),
            pltpu.SemaphoreType.DMA((channels // PER_COPY,)),
            pltpu.SemaphoreType.DMA((2,)),
        ],
        compiler_params=params(60),
        name="feature_lines",
    )(features, jnp.asarray(y_in), jnp.asarray(z_in))


def quad_of(channels):
    return 128 // channels


def chosen(shape, rule):
    row = lax.broadcasted_iota(jnp.int32, (shape[0], 1), 0)
    column = lax.broadcasted_iota(jnp.int32, (1, shape[1]), 1)
    return jnp.where(rule(row, column), 1.0, 0.0).astype(BF16)


def lane_order(lane, pairs, channels):
    per_group = pairs * CB
    return lax.rem(lane, per_group) // CB * channels + lane // per_group * CB + lax.rem(lane, CB)


def quad_columns(table, channels):
    quad = quad_of(channels)
    return table.reshape(-1, 2, KX // quad, quad).transpose(0, 3, 1, 2).reshape(table.shape)


def pack_kernel(w_ref, out_ref):
    pairs, _, kx, channels, _ = w_ref.shape
    quad = quad_of(channels)
    for k in range(pairs):
        for part in range(2):
            for t in range(kx // quad):
                out_ref[k, part, t] = jnp.concatenate([w_ref[k, part, t * quad + q] for q in range(quad)], axis=1)


def pack_weights(weight):
    pairs, _, kx, channels, _ = weight.shape
    quad = quad_of(channels)
    shape = (pairs, 2, kx // quad, channels, quad * channels)
    return pl.pallas_call(
        pack_kernel,
        grid=(pairs // PER_STEP,),
        in_specs=[pl.BlockSpec((PER_STEP,) + weight.shape[1:], lambda k: (k, 0, 0, 0, 0))],
        out_specs=pl.BlockSpec((PER_STEP,) + shape[1:], lambda k: (k, 0, 0, 0, 0)),
        out_shape=jax.ShapeDtypeStruct(shape, F32),
        compiler_params=params(53),
        cost_estimate=pl.CostEstimate(flops=0, bytes_accessed=8 * weight.size * quad, transcendentals=0),
        name="pack_weights",
    )(weight)


def columns(spec_ref, k, pairs, channels):
    groups = channels // CB
    per_group = pairs * CB
    return jnp.concatenate(
        [spec_ref[pl.ds(pl.multiple_of(g * per_group + k * CB, CB), CB), :] for g in range(groups)], axis=0
    )


def mix_kernel(
    scale_ref, lines_ref, w_hbm, x_in_ref, x_out_ref, out_ref, spec_ref, w_ref, wide_ref, rows_ref, sem
):
    pairs, _, turns, channels, lanes = w_ref.shape
    copy = pltpu.make_async_copy(w_hbm, w_ref, sem)
    copy.start()
    spec = exact_dot(lines_ref[...].reshape(x_in_ref.shape[0], -1).T, x_in_ref[...], ((1,), (0,)))
    spec_ref[...] = spec
    over = chosen((6 * KX, 2 * KX * channels), lambda row, lane: lax.rem(row, 2 * KX) == lane // channels)
    wide_ref[...] = dot(jnp.concatenate(split3(spec), axis=1), over)
    copy.wait()

    def step(k, carry):
        v = columns(wide_ref, k, pairs, channels)
        reals, imags = [], []
        for t in range(turns):
            vr, vi = v[:, t * lanes : (t + 1) * lanes], v[:, (turns + t) * lanes : (turns + t + 1) * lanes]
            wr, wi = w_ref[k, 0, t], w_ref[k, 1, t]
            reals.append(jnp.sum(vr * wr - vi * wi, axis=0, keepdims=True))
            imags.append(jnp.sum(vr * wi + vi * wr, axis=0, keepdims=True))
        rows_ref[k] = jnp.concatenate(reals + imags, axis=0)
        return carry

    lax.fori_loop(0, pairs, step, 0, unroll=2)
    mixed = jnp.concatenate(
        [
            jnp.concatenate([rows_ref[k, :, q * channels : (q + 1) * channels] for k in range(pairs)], axis=1)
            for q in range(lanes // channels)
        ],
        axis=0,
    )
    order = chosen((mixed.shape[1],) * 2, lambda row, lane: row == lane_order(lane, pairs, channels))
    parts = dot(jnp.concatenate(split3(mixed), axis=0), order)
    n = mixed.shape[0]
    placed = (parts[2 * n :] + parts[n : 2 * n]) + parts[:n]
    out_ref[...] = exact_dot(x_out_ref[...], placed * scale_ref[...], ((1,), (0,))).reshape(out_ref.shape)


def whole(shape):
    return pl.BlockSpec(shape, lambda k: (0,) * len(shape))


def mix_modes(lines, packed, scale, x_in, x_out):
    pairs, _, turns, channels, wide = packed.shape
    lanes = pairs * channels
    return pl.pallas_call(
        mix_kernel,
        in_specs=[in_vmem(), in_vmem(), in_hbm()] + [in_vmem()] * 2,
        out_specs=[in_vmem(), in_vmem()],
        out_shape=[jax.ShapeDtypeStruct(lines.shape, F32), jax.ShapeDtypeStruct((lanes, 2 * KX), F32)],
        scratch_shapes=[
            pltpu.VMEM(packed.shape, F32),
            pltpu.VMEM((lanes, 2 * turns * wide), F32),
            pltpu.VMEM((pairs, 2 * turns, wide), F32),
            pltpu.SemaphoreType.DMA,
        ],
        compiler_params=params(53),
        name="mix_modes",
    )(scale, lines, packed, jnp.asarray(x_in), jnp.asarray(quad_columns(x_out, channels)))


def adjoint_kernel(
    scale_ref, lines_ref, w_hbm, x_in_ref, x_out_ref, sums_ref, out_ref, dspec_ref,
    w_ref, rows_ref, prod_ref, sem,
):
    pairs, _, turns, channels, lanes = w_ref.shape
    copy = pltpu.make_async_copy(w_hbm, w_ref, sem)
    copy.start()
    placed = exact_dot(x_in_ref[...].T, lines_ref[...].reshape(x_in_ref.shape[0], -1), ((1,), (0,))) * scale_ref[...]
    n = placed.shape[0]
    order = chosen((placed.shape[1],) * 2, lambda row, lane: lane_order(row, pairs, channels) == lane)
    parts = dot(jnp.concatenate(split3(placed), axis=0), order)
    rows = (parts[2 * n :] + parts[n : 2 * n]) + parts[:n]
    per = 2 * turns
    for k in range(pairs):
        mine = rows[:, k * channels : (k + 1) * channels]
        dspec_ref[k] = mine
        rows_ref[k] = jnp.concatenate([mine[q * per : (q + 1) * per] for q in range(lanes // channels)], axis=1)
    copy.wait()
    half = per * lanes

    def step(k, carry):
        d = rows_ref[k]
        at = pl.ds(pl.multiple_of(k * channels, channels), channels)
        for t in range(turns):
            dr, di = d[t : t + 1], d[turns + t : turns + t + 1]
            wr, wi = w_ref[k, 0, t], w_ref[k, 1, t]
            for part, value in enumerate((dr * wr + di * wi, di * wr - dr * wi)):
                first = (part * turns + t) * lanes
                hi = value.astype(BF16)
                prod_ref[at, first : first + lanes] = hi
                prod_ref[at, half + first : half + first + lanes] = (value - hi.astype(F32)).astype(BF16)
        return carry

    lax.fori_loop(0, pairs, step, 0, unroll=2)
    fold = chosen(
        (2 * half, 2 * KX),
        lambda row, lane: lax.rem(row, half) // channels == lax.rem(lane, per) * (lanes // channels) + lane // per,
    )
    sums = dot(prod_ref[...], fold)
    cols = jnp.concatenate(
        [
            sums[k * channels + g * CB : k * channels + (g + 1) * CB]
            for g in range(channels // CB)
            for k in range(pairs)
        ],
        axis=0,
    )
    lines = exact_dot(x_out_ref[...], cols, ((1,), (1,)))
    out_ref[:, :, :, : lines.shape[1]] = lines.reshape(lines_ref.shape)
    out_ref[:, :, :, lines.shape[1] :] = jnp.broadcast_to(sums_ref[...][None], out_ref.shape[:1] + sums_ref.shape)


def adjoint_modes(lines, packed, scale, x_in, x_out, sums):
    pairs, _, turns, channels, wide = packed.shape
    return pl.pallas_call(
        adjoint_kernel,
        in_specs=[in_vmem(), in_vmem(), in_hbm()] + [in_vmem()] * 3,
        out_specs=[in_vmem(), in_vmem()],
        out_shape=[
            jax.ShapeDtypeStruct(lines.shape[:3] + (lines.shape[3] + sums.shape[2],), F32),
            jax.ShapeDtypeStruct((pairs, 2 * KX, channels), F32),
        ],
        scratch_shapes=[
            pltpu.VMEM(packed.shape, F32),
            pltpu.VMEM((pairs, 2 * turns, wide), F32),
            pltpu.VMEM((pairs * channels, 4 * turns * wide), BF16),
            pltpu.SemaphoreType.DMA,
        ],
        compiler_params=params(53),
        name="adjoint_modes",
    )(
        scale,
        lines,
        packed,
        jnp.asarray(quad_columns(x_in, channels)),
        jnp.asarray(quad_columns(x_out, channels)),
        sums,
    )


PER_STEP = 4


def outer_kernel(spec_ref, dspec_ref, out_ref):
    channels = dspec_ref.shape[-1]
    pairs = spec_ref.shape[0] // channels
    quad = quad_of(channels)
    per = 2 * KX // quad
    for i in range(PER_STEP):
        v = columns(spec_ref, pl.program_id(0) * PER_STEP + i, pairs, channels)
        d = dspec_ref[i]
        for a in range(KX):
            vr, vi = v[:, a : a + 1], v[:, KX + a : KX + a + 1]
            t, q = divmod(a, quad)
            dr = d[q * per + t : q * per + t + 1]
            di = d[q * per + per // 2 + t : q * per + per // 2 + t + 1]
            out_ref[i, 0, a] = vr * dr + vi * di
            out_ref[i, 1, a] = vr * di - vi * dr


def mode_gradient(spec, dspec):
    pairs, twice_kx, channels = dspec.shape
    shape = (pairs, 2, twice_kx // 2, channels, channels)
    return pl.pallas_call(
        outer_kernel,
        grid=(pairs // PER_STEP,),
        in_specs=[whole(spec.shape), pl.BlockSpec((PER_STEP, twice_kx, channels), lambda k: (k, 0, 0))],
        out_specs=pl.BlockSpec((PER_STEP,) + shape[1:], lambda k: (k, 0, 0, 0, 0)),
        out_shape=jax.ShapeDtypeStruct(shape, F32),
        compiler_params=params(24),
        name="mode_gradient",
    )(spec, dspec)


def spread(w, by_column, out_ref):
    n = out_ref.shape[0]
    fold = (
        lax.broadcasted_iota(jnp.int32, (n, w.shape[0]), 0) // YB
        == lax.broadcasted_iota(jnp.int32, (n, w.shape[0]), 1)
    ).astype(F32).astype(BF16)
    wide = lax.dot_general(fold, w, (((1,), (1 if by_column else 0,)), ((), ())), preferred_element_type=F32)
    full = lax.dot_general(wide.astype(BF16), fold, (((1,), (1,)), ((), ())), preferred_element_type=F32)
    same = lax.rem(lax.broadcasted_iota(jnp.int32, (n, n), 0), YB) == lax.rem(
        lax.broadcasted_iota(jnp.int32, (n, n), 1), YB
    )
    out_ref[...] = jnp.where(same, full, 0.0).astype(BF16)


def synthesise_y(lines_ref, bias, y_out_ref, low_ref, b_ref):
    rows = KY * 2 * XB
    lanes = KZ * CB
    ny = b_ref.shape[2]
    tables = y_out_ref[...].reshape(-1, rows)
    tables = jnp.concatenate([tables, tables], axis=1)
    for h in range(lines_ref.shape[1]):
        block = lines_ref[:, h, :, : low_ref.shape[1]].reshape(rows, low_ref.shape[1])
        if bias is not None:
            row = lax.broadcasted_iota(jnp.int32, (rows, 1), 0) // XB
            block = block + jnp.where(row == KY // 2 * 2, bias, 0.0)
        hi = block.astype(BF16)
        low_ref[:rows] = hi
        low_ref[rows:] = (block - hi.astype(F32)).astype(BF16)
        b = dot(tables, low_ref[...]).astype(BF16)
        for x in range(XB):
            for part in range(2):
                first = (2 * x + part) * ny
                for g in range(b_ref.shape[1]):
                    b_ref[h * XB + x, g, :, part * lanes : (part + 1) * lanes] = b[
                        first : first + ny, g * lanes : (g + 1) * lanes
                    ]


def channel_mix(kron, cells_ref, x, y):
    nz = cells_ref.shape[-1]
    tiles = [cells_ref[:, x, y + t * YB : y + (t + 1) * YB, :].reshape(-1, nz) for t in range(2)]
    return dot(kron, jnp.concatenate(tiles, axis=1))


def store_mix(kron_ref, cells_ref, out_ref):
    channels, rows, ny, nz = cells_ref.shape
    for x in range(rows):
        for y in range(0, ny, 2 * YB):
            local = channel_mix(kron_ref[...], cells_ref, x, y).astype(BF16)
            for t in range(2):
                out_ref[:, x, y + t * YB : y + (t + 1) * YB, :] = local[:, t * nz : (t + 1) * nz].reshape(
                    channels, YB, nz
                )


def local_kernel(by_column, cells_ref, w_ref, out_ref, kron_ref):
    @pl.when(pl.program_id(0) == 0)
    def _():
        spread(w_ref[...], by_column, kron_ref)

    store_mix(kron_ref, cells_ref, out_ref)


def local_branch(features, weight, by_column):
    channels, rows, ny, nz = features.shape
    cells = pl.BlockSpec((channels, 2, ny, nz), lambda x: (0, x, 0, 0))
    return pl.pallas_call(
        functools.partial(local_kernel, by_column),
        grid=(rows // 2,),
        in_specs=[cells, whole(weight.shape)],
        out_specs=cells,
        out_shape=jax.ShapeDtypeStruct(features.shape, BF16),
        scratch_shapes=[pltpu.VMEM((channels * YB, channels * YB), BF16)],
        compiler_params=params(53),
        cost_estimate=pl.CostEstimate(flops=2 * features.size * channels, bytes_accessed=4 * features.size, transcendentals=0),
        name="local_branch",
    )(features, weight)


ROOT = math.sqrt(2.0 / math.pi)
CUBE = 0.044715 * ROOT


def gelu_slope(u):
    square = u * u
    t = jnp.tanh(u * (ROOT + CUBE * square))
    inner = u * (0.5 * ROOT + 1.5 * CUBE * square)
    return (1.0 + t) * (0.5 + (1.0 - t) * inner)


def row_copy(src, dst, sem):
    return lambda x: pltpu.make_async_copy(src.at[:, x], dst.at[:, x], sem.at[x])


def each_row(rows, act):
    def step(x, carry):
        act(x)
        return carry

    lax.fori_loop(0, rows, step, 0)


def rows_in_turn(rows, z_out_ref, b_ref, even_ref, odd_ref, arrive, use, leave):
    groups = b_ref.shape[1]

    lanes = even_ref.shape[2] // CB * PER_USE

    def synthesise_z(x, g, c, space_ref):
        at = slice(c // PER_USE * lanes, (c // PER_USE + 1) * lanes)
        space_ref[g, :, at] = dot(b_ref[x, g], z_out_ref[:, at])

    for g in range(groups):
        for c in range(0, CB, PER_USE):
            synthesise_z(0, g, c, even_ref)

    def pair(i, carry):
        for n, here, there in ((0, even_ref, odd_ref), (1, odd_ref, even_ref)):
            x = 2 * i + n
            arrive(x)
            for g in range(groups):
                for c in range(0, CB, PER_USE):
                    synthesise_z(jnp.minimum(x + 1, rows - 1), g, c, there)
                    use(x, g, c, here)
            leave(x)
        return carry

    return pair


PER_USE = 8


def slope_kernel(
    bias_ref, lines_ref, local_hbm, cot_hbm, y_in_ref, z_in_ref, y_out_ref, z_out_ref, grad_hbm, out_ref,
    local_ref, cot_ref, grad_ref, low_ref, b_ref, even_ref, odd_ref, g_ref, local_sem, cot_sem, grad_sem,
):
    channels, rows, ny, nz = local_ref.shape
    local_copy = row_copy(local_hbm, local_ref, local_sem)
    cot_copy = row_copy(cot_hbm, cot_ref, cot_sem)
    grad_copy = row_copy(grad_ref, grad_hbm, grad_sem)

    def begin(x):
        local_copy(x).start()
        cot_copy(x).start()

    each_row(2, begin)
    synthesise_y(lines_ref, bias_ref[...], y_out_ref, low_ref, b_ref)

    def arrive(x):
        local_copy(x).wait()
        cot_copy(x).wait()

        @pl.when(x + 2 < rows)
        def _():
            begin(x + 2)

    def use(x, g, first, space_ref):
        for c in range(first, first + PER_USE):
            o = g * CB + c
            for y in range(0, ny, YB):
                at = slice(y, y + YB)
                u = space_ref[g, at, c * nz : (c + 1) * nz] + local_ref[o, x, at, :].astype(F32)
                grad_ref[o, x, at, :] = (gelu_slope(u) * cot_ref[o, x, at, :].astype(F32)).astype(BF16)

    pair = rows_in_turn(rows, z_out_ref, b_ref, even_ref, odd_ref, arrive, use, lambda x: grad_copy(x).start())

    def block(h):
        lax.fori_loop(h * XB // 2, (h + 1) * XB // 2, pair, 0)
        analyse_y(
            lambda c: grad_ref[c, pl.ds(h * XB, XB)].reshape(XB * ny, nz), 0, channels, y_in_ref[...], g_ref
        )
        total = analyse_z(z_in_ref, g_ref)
        put_lines(out_ref, h, 0, total)

    each_row(rows // XB, block)
    each_row(rows, lambda x: grad_copy(x).wait())


def space_scratch(rows, channels, ny, nz):
    groups = channels // CB
    return [
        pltpu.VMEM((2 * KY * 2 * XB, KZ * channels), BF16),
        pltpu.VMEM((rows, groups, ny, 2 * KZ * CB), BF16),
        pltpu.VMEM((groups, ny, CB * nz), F32),
        pltpu.VMEM((groups, ny, CB * nz), F32),
    ]


def slope(lines, local, cotangent, biases):
    channels, rows, ny, nz = local.shape
    y_in, z_in, y_out, z_out = plane_tables(ny, nz)
    lanes = KZ * channels
    bias_lanes = jnp.where(jnp.arange(KZ)[None, :, None] == 0, biases.reshape(-1, 1, CB), 0.0).reshape(1, lanes)
    return pl.pallas_call(
        slope_kernel,
        in_specs=[in_vmem(), in_vmem(), in_hbm(), in_hbm()] + [in_vmem()] * 4,
        out_specs=[in_hbm(), in_vmem()],
        out_shape=[
            jax.ShapeDtypeStruct(local.shape, BF16),
            jax.ShapeDtypeStruct((KY, rows // XB, 2 * XB, lanes), F32),
        ],
        scratch_shapes=[pltpu.VMEM(local.shape, BF16)] * 3
        + space_scratch(rows, channels, ny, nz)
        + [pltpu.VMEM((channels // CB * KY * 2 * XB, CB * 2 * nz), BF16)]
        + [pltpu.SemaphoreType.DMA((rows,))] * 3,
        compiler_params=params(44),
        name="slope",
    )(bias_lanes, lines, local, cotangent, jnp.asarray(y_in), jnp.asarray(z_in), jnp.asarray(y_out), jnp.asarray(z_out))


def back_kernel(
    factor, apart, lines_ref, *refs
):
    sums_ref, refs = (refs[0], refs[1:]) if apart else (None, refs)
    (
        local_hbm, y_out_ref, z_out_ref, out_hbm, mix_ref, bias_ref,
        local_ref, out_ref, low_ref, b_ref, even_ref, odd_ref, local_sem, out_sem,
    ) = refs
    channels, rows, ny, nz = local_ref.shape
    local_copy = row_copy(local_hbm, local_ref, local_sem)
    out_copy = row_copy(out_ref, out_hbm, out_sem)
    each_row(3, lambda x: local_copy(x).start())
    synthesise_y(lines_ref, None, y_out_ref, low_ref, b_ref)
    wide = channels * channels // 8
    shared = sums_ref[...] if apart else lines_ref[:, :, :, low_ref.shape[1] :]
    total = jnp.sum(shared, axis=0) * factor
    mixing, biases = total[0, :, :wide], total[-1, :, total.shape[2] - wide :]
    mix_ref[...] = jnp.concatenate([mixing[:, c : c + channels] for c in range(0, wide, channels)], axis=0)
    bias_ref[...] = biases[:1, :channels]

    def arrive(x):
        local_copy(x).wait()

        @pl.when(x + 3 < rows)
        def _():
            local_copy(x + 3).start()

    def use(x, g, first, space_ref):
        for c in range(first, first + PER_USE):
            o = g * CB + c
            for y in range(0, ny, YB):
                at = slice(y, y + YB)
                u = space_ref[g, at, c * nz : (c + 1) * nz] + local_ref[o, x, at, :].astype(F32)
                out_ref[o, x, at, :] = u.astype(BF16)

    pair = rows_in_turn(rows, z_out_ref, b_ref, even_ref, odd_ref, arrive, use, lambda x: out_copy(x).start())
    lax.fori_loop(0, rows // 2, pair, 0)
    each_row(rows, lambda x: out_copy(x).wait())


def back(lines, sums, local, factor):
    apart = sums is not None
    channels, rows, ny, nz = local.shape
    _, _, y_out, z_out = plane_tables(ny, nz)
    return pl.pallas_call(
        functools.partial(back_kernel, factor, apart),
        in_specs=[in_vmem()] * (1 + apart) + [in_hbm(), in_vmem(), in_vmem()],
        out_specs=[in_hbm(), in_vmem(), in_vmem()],
        out_shape=[
            jax.ShapeDtypeStruct(local.shape, BF16),
            jax.ShapeDtypeStruct((channels, channels), F32),
            jax.ShapeDtypeStruct((1, channels), F32),
        ],
        scratch_shapes=[pltpu.VMEM(local.shape, BF16)] * 2
        + space_scratch(rows, channels, ny, nz)
        + [pltpu.SemaphoreType.DMA((rows,))] * 2,
        compiler_params=params(46),
        name="back",
    )(lines, *([sums] if apart else []), local, jnp.asarray(y_out), jnp.asarray(z_out))


def cell_sums_kernel(grad_ref, f_ref, dlines_ref, sums_ref, acc_ref):
    step = pl.program_id(0)
    channels, rows, ny, nz = f_ref.shape
    lanes = KZ * CB

    @pl.when(step == 0)
    def _():
        acc_ref[...] = jnp.zeros_like(acc_ref)

    def tiles(ref):
        return jnp.concatenate(
            [ref[:, x, y : y + YB, :].reshape(-1, nz) for x in range(rows) for y in range(0, ny, YB)], axis=1
        )

    acc_ref[...] += lax.dot_general(tiles(grad_ref), tiles(f_ref), (((1,), (1,)), ((), ())), preferred_element_type=F32)

    @pl.when(step == pl.num_programs(0) - 1)
    def _():
        n = channels * YB
        same = lax.rem(lax.broadcasted_iota(jnp.int32, (n, n), 0), YB) == lax.rem(
            lax.broadcasted_iota(jnp.int32, (n, n), 1), YB
        )
        picked = jnp.where(same, acc_ref[...], 0.0)
        fold = (
            lax.broadcasted_iota(jnp.int32, (channels, n), 1) // YB
            == lax.broadcasted_iota(jnp.int32, (channels, n), 0)
        ).astype(F32)
        half = exact_dot(fold, picked, ((1,), (0,)))
        mixing = exact_dot(half, fold, ((1,), (1,)))
        zero = dlines_ref[KY // 2].reshape(-1, KZ * channels)
        real = lax.rem(lax.broadcasted_iota(jnp.int32, (zero.shape[0], 1), 0), 2 * XB) < XB
        line = jnp.sum(jnp.where(real, zero, 0.0), axis=0, keepdims=True)
        lane = lax.broadcasted_iota(jnp.int32, (channels, KZ * channels), 1)
        channel = lax.broadcasted_iota(jnp.int32, (channels, KZ * channels), 0)
        pick = (lane == channel // CB * lanes + lax.rem(channel, CB)).astype(F32)
        biases = exact_dot(jnp.broadcast_to(line, (8, line.shape[1])), pick, ((1,), (1,)))
        packed = [
            jnp.concatenate([mixing[r : r + 8] for r in range(0, channels, 8)], axis=1),
            jnp.concatenate([biases] * (channels // 8), axis=1),
        ]
        if sums_ref.shape[0] == 1:
            sums_ref[0] = jnp.concatenate(packed, axis=1)
        else:
            for h in range(sums_ref.shape[0]):
                sums_ref[h] = packed[min(h, 1)]


def cell_sums(pre_grad, features, dlines):
    channels, rows, ny, nz = features.shape
    cells = pl.BlockSpec((channels, 2, ny, nz), lambda x: (0, x, 0, 0))
    tile = channels * YB
    blocks = rows // XB
    shape = (blocks, 8, channels * channels // 8 * (2 if blocks == 1 else 1))
    return pl.pallas_call(
        cell_sums_kernel,
        grid=(rows // 2,),
        in_specs=[cells, cells, whole(dlines.shape)],
        out_specs=whole(shape),
        out_shape=jax.ShapeDtypeStruct(shape, F32),
        scratch_shapes=[pltpu.VMEM((tile, tile), F32)],
        compiler_params=params(53),
        name="cell_sums",
    )(pre_grad, features, dlines)


def swap(blocks):
    return lax.all_to_all(blocks, "mp", 0, 0, tiled=True)


def shards(features, cotangent, spectral_weight, pointwise_weight, biases):
    channels, rows, ny, nz = features.shape
    devices = lax.axis_size("mp")
    nx = rows * devices
    pairs = spectral_weight.shape[0]
    groups = channels // CB
    blocks = rows // XB
    cut = KZ // pairs
    cells = nx * ny * nz
    x_in, x_out = line_tables(nx)
    if cut == 1:
        first_k = 0
    else:
        first_k = lax.rem(lax.axis_index("mp"), cut) * pairs
    ks = jnp.broadcast_to(jnp.arange(pairs)[None, :, None] + first_k, (groups, pairs, CB)).reshape(1, -1)
    scale = jnp.where(ks == 0, 1.0, 2.0).astype(F32) / float(cells)

    def to_owner(lines):
        if cut > 1:
            lines = lines.reshape(KY, blocks, 2 * XB, groups, cut, pairs * CB)
            lines = lines.transpose(0, 4, 1, 2, 3, 5)
        return swap(lines.reshape(devices, blocks, 2 * XB, -1))

    def to_cells(lines):
        lines = swap(lines)
        own = pairs * channels
        extra = None
        if cut > 1:
            extra = lines[..., own:]
            lines = lines[..., :own].reshape(KY, cut, blocks, 2 * XB, groups, pairs * CB)
            lines = lines.transpose(0, 2, 3, 4, 1, 5).reshape(KY, blocks, 2 * XB, -1)
        return lines, extra

    lines = to_owner(feature_lines(features))
    packed = pack_weights(spectral_weight)
    lines, packed = lax.optimization_barrier((lines, packed))
    mixed, spec = mix_modes(lines, packed, scale, x_in, x_out)
    pre_grad, dlines = slope(to_cells(mixed)[0], local_branch(features, pointwise_weight, False), cotangent, biases)
    sums = cell_sums(pre_grad, features, dlines)
    dlines = to_owner(dlines)
    dmixed, dspec = adjoint_modes(dlines, packed, scale, x_in, x_out, sums)
    back_lines, sums = to_cells(dmixed)
    spectral_grad = mode_gradient(spec, dspec)
    late_grad, _ = lax.optimization_barrier((pre_grad, dspec))
    local_back = local_branch(late_grad, pointwise_weight, True)
    features_grad, mix_total, bias_total = back(back_lines, sums, local_back, float(cells) ** -0.5)
    return (features_grad, spectral_grad, mix_total, bias_total[0])


def solution(mesh):
    return jax.shard_map(
        shards,
        mesh=mesh,
        in_specs=(
            P(None, ("groups", "mp"), None, None),
            P(None, ("groups", "mp"), None, None),
            P("mp", None, None, None, None),
            P(),
            P(),
        ),
        out_specs=(
            P(None, ("groups", "mp"), None, None),
            P(("groups", "mp"), None, None, None, None),
            P("groups", None),
            P("groups"),
        ),
        check_vma=False,
    )
```

```python
import functools
import math

import jax
import jax.numpy as jnp
import ml_dtypes
import numpy as np
from jax import lax
from jax.experimental import pallas as pl
from jax.experimental.pallas import tpu as pltpu
from jax.sharding import PartitionSpec as P

KX = 16
KY = 16
KZ = 16
XB = 4
CB = 8
YB = 16
MIB = 1 << 20

F32 = jnp.float32
BF16 = jnp.bfloat16


def angles(length, modes, signed):
    freqs = np.arange(modes) - (modes // 2 if signed else 0)
    theta = (np.arange(length)[:, None] * freqs[None, :] % length) * (2.0 * math.pi / length)
    return np.cos(theta), np.sin(theta)


def bf16(table):
    return np.asarray(table, np.float32).astype(ml_dtypes.bfloat16)


@functools.cache
def plane_tables(ny, nz):
    yc, ys = angles(ny, KY, True)
    zc, zs = angles(nz, KZ, False)
    eye_x = np.eye(XB)
    rows = np.stack([np.stack([yc, -ys], 0), np.stack([-ys, -yc], 0)], 0)
    y_in = np.einsum("mryj,xw->mjrxwy", rows, eye_x).reshape(2 * KY * 2 * XB, XB * ny)
    z_in = np.einsum("mzk,cd->cmzkd", np.stack([zc, zs], 0), np.eye(CB)).reshape(CB, 2 * nz, KZ * CB)
    mix = np.stack([np.stack([yc, -ys], 0), np.stack([ys, yc], 0)], 0)
    y_out = np.einsum("qryj,xw->xqyjrw", mix, eye_x).reshape(XB, 2 * ny, KY * 2 * XB)
    z_out = np.einsum("qzk,cd->qkcdz", np.stack([zc, -zs], 0), np.eye(CB)).reshape(2 * KZ * CB, CB * nz)
    return bf16(y_in), bf16(z_in), bf16(y_out), bf16(z_out)


@functools.cache
def line_tables(nx):
    xc, xs = angles(nx, KX, True)
    inward = np.stack([np.stack([xc, -xs], 1), np.stack([xs, xc], 1)], 0)
    outward = np.stack([np.stack([xc, -xs], 1), np.stack([xs, xc], 1)], 0)
    blocks = nx // XB

    def order(table):
        return (
            table.reshape(2, blocks, XB, 2 * KX)
            .transpose(1, 0, 2, 3)
            .reshape(nx * 2, 2 * KX)
            .astype(np.float32)
        )

    return order(inward), order(outward)


def params(mib):
    return pltpu.CompilerParams(vmem_limit_bytes=mib * MIB)


def exact_dot(a, b, dims):
    return lax.dot_general(a, b, (dims, ((), ())), precision=lax.Precision.HIGHEST, preferred_element_type=F32)


def dot(a, b):
    return jnp.dot(a, b, preferred_element_type=F32)


def split3(v):
    hi = v.astype(BF16)
    rest = v - hi.astype(F32)
    mid = rest.astype(BF16)
    return hi, mid, (rest - mid.astype(F32)).astype(BF16)


def analyse_y(planes, first, count, y_in, g_ref):
    rows = y_in.shape[0] // 2
    for c in range(first, first + count, 2):
        pair = jnp.concatenate([planes(c), planes(c + 1)], axis=1)
        nz = pair.shape[1] // 2
        g = dot(y_in, pair).astype(BF16)
        for i in range(2):
            group, of_group = divmod(c + i, CB)
            for m in range(2):
                g_ref[group * rows : (group + 1) * rows, (2 * of_group + m) * nz : (2 * of_group + m + 1) * nz] = g[
                    m * rows : (m + 1) * rows, i * nz : (i + 1) * nz
                ]


def analyse_z(z_in_ref, g_ref):
    return dot(g_ref[...], z_in_ref[...].reshape(g_ref.shape[1], -1))


def put_lines(out_ref, h, first_group, total):
    rows, lanes = KY * 2 * XB, total.shape[1]
    for g in range(total.shape[0] // rows):
        first = (first_group + g) * lanes
        out_ref[:, h, :, first : first + lanes] = total[g * rows : (g + 1) * rows].reshape(KY, 2 * XB, lanes)


def in_hbm():
    return pl.BlockSpec(memory_space=pltpu.HBM)


def in_vmem():
    return pl.BlockSpec(memory_space=pltpu.VMEM)


DEPTH = 2
PER_COPY = 8
PER_DOT = 16


def lines_kernel(f_hbm, y_in_hbm, z_in_hbm, out_ref, f_ref, g_ref, y_in_ref, z_in_ref, sem, table_sem):
    channels, rows, ny, nz = f_ref.shape
    copies = [
        pltpu.make_async_copy(f_hbm.at[pl.ds(c, PER_COPY)], f_ref.at[pl.ds(c, PER_COPY)], sem.at[c // PER_COPY])
        for c in range(0, channels, PER_COPY)
    ]
    tables = [
        pltpu.make_async_copy(y_in_hbm, y_in_ref, table_sem.at[0]),
        pltpu.make_async_copy(z_in_hbm, z_in_ref, table_sem.at[1]),
    ]
    tables[0].start()
    for copy in copies[:DEPTH]:
        copy.start()
    tables[1].start()
    tables[0].wait()
    y_in = y_in_ref[...]
    for first in range(0, channels, PER_DOT):
        for c in range(0, PER_DOT, PER_COPY):
            n = (first + c) // PER_COPY
            copies[n].wait()
            if n + DEPTH < len(copies):
                copies[n + DEPTH].start()
            for h in range(rows // XB):
                analyse_y(
                    lambda i: f_ref[first + i, h * XB : (h + 1) * XB].reshape(XB * ny, nz), c, PER_COPY, y_in, g_ref.at[h]
                )
        if first == 0:
            tables[1].wait()
        for h in range(rows // XB):
            put_lines(out_ref, h, first // CB, analyse_z(z_in_ref, g_ref.at[h]))


def feature_lines(features):
    channels, rows, ny, nz = features.shape
    y_in, z_in, _, _ = plane_tables(ny, nz)
    blocks = rows // XB
    return pl.pallas_call(
        lines_kernel,
        in_specs=[in_hbm()] * 3,
        out_specs=in_vmem(),
        out_shape=jax.ShapeDtypeStruct((KY, blocks, 2 * XB, KZ * channels), F32),
        scratch_shapes=[
            pltpu.VMEM(features.shape, BF16),
            pltpu.VMEM((blocks, PER_DOT // CB * KY * 2 * XB, CB * 2 * nz), BF16),
            pltpu.VMEM(y_in.shape, BF16),
            pltpu.VMEM(z_in.shape, BF16),
            pltpu.SemaphoreType.DMA((channels // PER_COPY,)),
            pltpu.SemaphoreType.DMA((2,)),
        ],
        compiler_params=params(60),
        name="feature_lines",
    )(features, jnp.asarray(y_in), jnp.asarray(z_in))


def quad_of(channels):
    return 128 // channels


def chosen(shape, rule):
    row = lax.broadcasted_iota(jnp.int32, (shape[0], 1), 0)
    column = lax.broadcasted_iota(jnp.int32, (1, shape[1]), 1)
    return jnp.where(rule(row, column), 1.0, 0.0).astype(BF16)


def lane_order(lane, pairs, channels):
    per_group = pairs * CB
    return lax.rem(lane, per_group) // CB * channels + lane // per_group * CB + lax.rem(lane, CB)


def quad_columns(table, channels):
    quad = quad_of(channels)
    return table.reshape(-1, 2, KX // quad, quad).transpose(0, 3, 1, 2).reshape(table.shape)


def pack_kernel(w_ref, out_ref):
    pairs, _, kx, channels, _ = w_ref.shape
    quad = quad_of(channels)
    for k in range(pairs):
        for part in range(2):
            for t in range(kx // quad):
                out_ref[k, part, t] = jnp.concatenate([w_ref[k, part, t * quad + q] for q in range(quad)], axis=1)


def pack_weights(weight):
    pairs, _, kx, channels, _ = weight.shape
    quad = quad_of(channels)
    shape = (pairs, 2, kx // quad, channels, quad * channels)
    return pl.pallas_call(
        pack_kernel,
        grid=(pairs // PER_STEP,),
        in_specs=[pl.BlockSpec((PER_STEP,) + weight.shape[1:], lambda k: (k, 0, 0, 0, 0))],
        out_specs=pl.BlockSpec((PER_STEP,) + shape[1:], lambda k: (k, 0, 0, 0, 0)),
        out_shape=jax.ShapeDtypeStruct(shape, F32),
        compiler_params=params(53),
        cost_estimate=pl.CostEstimate(flops=0, bytes_accessed=8 * weight.size * quad, transcendentals=0),
        name="pack_weights",
    )(weight)


def columns(spec_ref, k, pairs, channels):
    groups = channels // CB
    per_group = pairs * CB
    return jnp.concatenate(
        [spec_ref[pl.ds(pl.multiple_of(g * per_group + k * CB, CB), CB), :] for g in range(groups)], axis=0
    )


def mix_kernel(
    scale_ref, lines_ref, w_hbm, x_in_ref, x_out_ref, out_ref, spec_ref, w_ref, wide_ref, rows_ref, sem
):
    pairs, _, turns, channels, lanes = w_ref.shape
    copy = pltpu.make_async_copy(w_hbm, w_ref, sem)
    copy.start()
    spec = exact_dot(lines_ref[...].reshape(x_in_ref.shape[0], -1).T, x_in_ref[...], ((1,), (0,)))
    spec_ref[...] = spec
    over = chosen((6 * KX, 2 * KX * channels), lambda row, lane: lax.rem(row, 2 * KX) == lane // channels)
    wide_ref[...] = dot(jnp.concatenate(split3(spec), axis=1), over)
    copy.wait()

    def step(k, carry):
        v = columns(wide_ref, k, pairs, channels)
        reals, imags = [], []
        for t in range(turns):
            vr, vi = v[:, t * lanes : (t + 1) * lanes], v[:, (turns + t) * lanes : (turns + t + 1) * lanes]
            wr, wi = w_ref[k, 0, t], w_ref[k, 1, t]
            reals.append(jnp.sum(vr * wr - vi * wi, axis=0, keepdims=True))
            imags.append(jnp.sum(vr * wi + vi * wr, axis=0, keepdims=True))
        rows_ref[k] = jnp.concatenate(reals + imags, axis=0)
        return carry

    lax.fori_loop(0, pairs, step, 0, unroll=2)
    mixed = jnp.concatenate(
        [
            jnp.concatenate([rows_ref[k, :, q * channels : (q + 1) * channels] for k in range(pairs)], axis=1)
            for q in range(lanes // channels)
        ],
        axis=0,
    )
    order = chosen((mixed.shape[1],) * 2, lambda row, lane: row == lane_order(lane, pairs, channels))
    parts = dot(jnp.concatenate(split3(mixed), axis=0), order)
    n = mixed.shape[0]
    placed = (parts[2 * n :] + parts[n : 2 * n]) + parts[:n]
    out_ref[...] = exact_dot(x_out_ref[...], placed * scale_ref[...], ((1,), (0,))).reshape(out_ref.shape)


def whole(shape):
    return pl.BlockSpec(shape, lambda k: (0,) * len(shape))


def mix_modes(lines, packed, scale, x_in, x_out):
    pairs, _, turns, channels, wide = packed.shape
    lanes = pairs * channels
    return pl.pallas_call(
        mix_kernel,
        in_specs=[in_vmem(), in_vmem(), in_hbm()] + [in_vmem()] * 2,
        out_specs=[in_vmem(), in_vmem()],
        out_shape=[jax.ShapeDtypeStruct(lines.shape, F32), jax.ShapeDtypeStruct((lanes, 2 * KX), F32)],
        scratch_shapes=[
            pltpu.VMEM(packed.shape, F32),
            pltpu.VMEM((lanes, 2 * turns * wide), F32),
            pltpu.VMEM((pairs, 2 * turns, wide), F32),
            pltpu.SemaphoreType.DMA,
        ],
        compiler_params=params(46),
        name="mix_modes",
    )(scale, lines, packed, jnp.asarray(x_in), jnp.asarray(quad_columns(x_out, channels)))


def adjoint_kernel(
    scale_ref, lines_ref, w_hbm, x_in_ref, x_out_ref, sums_ref, out_ref, dspec_ref,
    w_ref, rows_ref, prod_ref, sem,
):
    pairs, _, turns, channels, lanes = w_ref.shape
    copy = pltpu.make_async_copy(w_hbm, w_ref, sem)
    copy.start()
    placed = exact_dot(x_in_ref[...].T, lines_ref[...].reshape(x_in_ref.shape[0], -1), ((1,), (0,))) * scale_ref[...]
    n = placed.shape[0]
    order = chosen((placed.shape[1],) * 2, lambda row, lane: lane_order(row, pairs, channels) == lane)
    parts = dot(jnp.concatenate(split3(placed), axis=0), order)
    rows = (parts[2 * n :] + parts[n : 2 * n]) + parts[:n]
    per = 2 * turns
    for k in range(pairs):
        mine = rows[:, k * channels : (k + 1) * channels]
        dspec_ref[k] = mine
        rows_ref[k] = jnp.concatenate([mine[q * per : (q + 1) * per] for q in range(lanes // channels)], axis=1)
    copy.wait()
    half = per * lanes

    def step(k, carry):
        d = rows_ref[k]
        at = pl.ds(pl.multiple_of(k * channels, channels), channels)
        for t in range(turns):
            dr, di = d[t : t + 1], d[turns + t : turns + t + 1]
            wr, wi = w_ref[k, 0, t], w_ref[k, 1, t]
            for part, value in enumerate((dr * wr + di * wi, di * wr - dr * wi)):
                first = (part * turns + t) * lanes
                hi = value.astype(BF16)
                prod_ref[at, first : first + lanes] = hi
                prod_ref[at, half + first : half + first + lanes] = (value - hi.astype(F32)).astype(BF16)
        return carry

    lax.fori_loop(0, pairs, step, 0, unroll=2)
    fold = chosen(
        (2 * half, 2 * KX),
        lambda row, lane: lax.rem(row, half) // channels == lax.rem(lane, per) * (lanes // channels) + lane // per,
    )
    sums = dot(prod_ref[...], fold)
    cols = jnp.concatenate(
        [
            sums[k * channels + g * CB : k * channels + (g + 1) * CB]
            for g in range(channels // CB)
            for k in range(pairs)
        ],
        axis=0,
    )
    lines = exact_dot(x_out_ref[...], cols, ((1,), (1,)))
    out_ref[:, :, :, : lines.shape[1]] = lines.reshape(lines_ref.shape)
    out_ref[:, :, :, lines.shape[1] :] = jnp.broadcast_to(sums_ref[...][None], out_ref.shape[:1] + sums_ref.shape)


def adjoint_modes(lines, packed, scale, x_in, x_out, sums):
    pairs, _, turns, channels, wide = packed.shape
    return pl.pallas_call(
        adjoint_kernel,
        in_specs=[in_vmem(), in_vmem(), in_hbm()] + [in_vmem()] * 3,
        out_specs=[in_vmem(), in_vmem()],
        out_shape=[
            jax.ShapeDtypeStruct(lines.shape[:3] + (lines.shape[3] + sums.shape[2],), F32),
            jax.ShapeDtypeStruct((pairs, 2 * KX, channels), F32),
        ],
        scratch_shapes=[
            pltpu.VMEM(packed.shape, F32),
            pltpu.VMEM((pairs, 2 * turns, wide), F32),
            pltpu.VMEM((pairs * channels, 4 * turns * wide), BF16),
            pltpu.SemaphoreType.DMA,
        ],
        compiler_params=params(53),
        name="adjoint_modes",
    )(
        scale,
        lines,
        packed,
        jnp.asarray(quad_columns(x_in, channels)),
        jnp.asarray(quad_columns(x_out, channels)),
        sums,
    )


PER_STEP = 4


def outer_kernel(spec_ref, dspec_ref, out_ref):
    channels = dspec_ref.shape[-1]
    pairs = spec_ref.shape[0] // channels
    quad = quad_of(channels)
    per = 2 * KX // quad
    for i in range(PER_STEP):
        v = columns(spec_ref, pl.program_id(0) * PER_STEP + i, pairs, channels)
        d = dspec_ref[i]
        for a in range(KX):
            vr, vi = v[:, a : a + 1], v[:, KX + a : KX + a + 1]
            t, q = divmod(a, quad)
            dr = d[q * per + t : q * per + t + 1]
            di = d[q * per + per // 2 + t : q * per + per // 2 + t + 1]
            out_ref[i, 0, a] = vr * dr + vi * di
            out_ref[i, 1, a] = vr * di - vi * dr


def mode_gradient(spec, dspec):
    pairs, twice_kx, channels = dspec.shape
    shape = (pairs, 2, twice_kx // 2, channels, channels)
    return pl.pallas_call(
        outer_kernel,
        grid=(pairs // PER_STEP,),
        in_specs=[whole(spec.shape), pl.BlockSpec((PER_STEP, twice_kx, channels), lambda k: (k, 0, 0))],
        out_specs=pl.BlockSpec((PER_STEP,) + shape[1:], lambda k: (k, 0, 0, 0, 0)),
        out_shape=jax.ShapeDtypeStruct(shape, F32),
        compiler_params=params(24),
        name="mode_gradient",
    )(spec, dspec)


def spread(w, by_column, out_ref):
    n = out_ref.shape[0]
    fold = (
        lax.broadcasted_iota(jnp.int32, (n, w.shape[0]), 0) // YB
        == lax.broadcasted_iota(jnp.int32, (n, w.shape[0]), 1)
    ).astype(F32).astype(BF16)
    wide = lax.dot_general(fold, w, (((1,), (1 if by_column else 0,)), ((), ())), preferred_element_type=F32)
    full = lax.dot_general(wide.astype(BF16), fold, (((1,), (1,)), ((), ())), preferred_element_type=F32)
    same = lax.rem(lax.broadcasted_iota(jnp.int32, (n, n), 0), YB) == lax.rem(
        lax.broadcasted_iota(jnp.int32, (n, n), 1), YB
    )
    out_ref[...] = jnp.where(same, full, 0.0).astype(BF16)


def synthesise_y(lines_ref, bias, y_out_ref, low_ref, b_ref):
    rows = KY * 2 * XB
    lanes = KZ * CB
    ny = b_ref.shape[2]
    tables = y_out_ref[...].reshape(-1, rows)
    tables = jnp.concatenate([tables, tables], axis=1)
    for h in range(lines_ref.shape[1]):
        block = lines_ref[:, h, :, : low_ref.shape[1]].reshape(rows, low_ref.shape[1])
        if bias is not None:
            row = lax.broadcasted_iota(jnp.int32, (rows, 1), 0) // XB
            block = block + jnp.where(row == KY // 2 * 2, bias, 0.0)
        hi = block.astype(BF16)
        low_ref[:rows] = hi
        low_ref[rows:] = (block - hi.astype(F32)).astype(BF16)
        b = dot(tables, low_ref[...]).astype(BF16)
        for x in range(XB):
            for part in range(2):
                first = (2 * x + part) * ny
                for g in range(b_ref.shape[1]):
                    b_ref[h * XB + x, g, :, part * lanes : (part + 1) * lanes] = b[
                        first : first + ny, g * lanes : (g + 1) * lanes
                    ]


def channel_mix(kron, cells_ref, x, y):
    nz = cells_ref.shape[-1]
    tiles = [cells_ref[:, x, y + t * YB : y + (t + 1) * YB, :].reshape(-1, nz) for t in range(2)]
    return dot(kron, jnp.concatenate(tiles, axis=1))


def store_mix(kron_ref, cells_ref, out_ref):
    channels, rows, ny, nz = cells_ref.shape
    for x in range(rows):
        for y in range(0, ny, 2 * YB):
            local = channel_mix(kron_ref[...], cells_ref, x, y).astype(BF16)
            for t in range(2):
                out_ref[:, x, y + t * YB : y + (t + 1) * YB, :] = local[:, t * nz : (t + 1) * nz].reshape(
                    channels, YB, nz
                )


def local_kernel(by_column, cells_ref, w_ref, out_ref, kron_ref):
    @pl.when(pl.program_id(0) == 0)
    def _():
        spread(w_ref[...], by_column, kron_ref)

    store_mix(kron_ref, cells_ref, out_ref)


def local_branch(features, weight, by_column):
    channels, rows, ny, nz = features.shape
    cells = pl.BlockSpec((channels, 2, ny, nz), lambda x: (0, x, 0, 0))
    return pl.pallas_call(
        functools.partial(local_kernel, by_column),
        grid=(rows // 2,),
        in_specs=[cells, whole(weight.shape)],
        out_specs=cells,
        out_shape=jax.ShapeDtypeStruct(features.shape, BF16),
        scratch_shapes=[pltpu.VMEM((channels * YB, channels * YB), BF16)],
        compiler_params=params(53),
        cost_estimate=pl.CostEstimate(flops=2 * features.size * channels, bytes_accessed=4 * features.size, transcendentals=0),
        name="local_branch",
    )(features, weight)


ROOT = math.sqrt(2.0 / math.pi)
CUBE = 0.044715 * ROOT


def gelu_slope(u):
    square = u * u
    t = jnp.tanh(u * (ROOT + CUBE * square))
    inner = u * (0.5 * ROOT + 1.5 * CUBE * square)
    return (1.0 + t) * (0.5 + (1.0 - t) * inner)


def row_copy(src, dst, sem):
    return lambda x: pltpu.make_async_copy(src.at[:, x], dst.at[:, x], sem.at[x])


def each_row(rows, act):
    def step(x, carry):
        act(x)
        return carry

    lax.fori_loop(0, rows, step, 0)


def rows_in_turn(rows, z_out_ref, b_ref, even_ref, odd_ref, arrive, use, leave):
    groups = b_ref.shape[1]

    lanes = even_ref.shape[2] // CB * PER_USE

    def synthesise_z(x, g, c, space_ref):
        at = slice(c // PER_USE * lanes, (c // PER_USE + 1) * lanes)
        space_ref[g, :, at] = dot(b_ref[x, g], z_out_ref[:, at])

    for g in range(groups):
        for c in range(0, CB, PER_USE):
            synthesise_z(0, g, c, even_ref)

    def pair(i, carry):
        for n, here, there in ((0, even_ref, odd_ref), (1, odd_ref, even_ref)):
            x = 2 * i + n
            arrive(x)
            for g in range(groups):
                for c in range(0, CB, PER_USE):
                    synthesise_z(jnp.minimum(x + 1, rows - 1), g, c, there)
                    use(x, g, c, here)
            leave(x)
        return carry

    return pair


PER_USE = 8


def slope_kernel(
    bias_ref, lines_ref, local_hbm, cot_hbm, y_in_ref, z_in_ref, y_out_ref, z_out_ref, grad_hbm, out_ref,
    local_ref, cot_ref, grad_ref, low_ref, b_ref, even_ref, odd_ref, g_ref, local_sem, cot_sem, grad_sem,
):
    channels, rows, ny, nz = local_ref.shape
    local_copy = row_copy(local_hbm, local_ref, local_sem)
    cot_copy = row_copy(cot_hbm, cot_ref, cot_sem)
    grad_copy = row_copy(grad_ref, grad_hbm, grad_sem)

    def begin(x):
        local_copy(x).start()
        cot_copy(x).start()

    each_row(2, begin)
    synthesise_y(lines_ref, bias_ref[...], y_out_ref, low_ref, b_ref)

    def arrive(x):
        local_copy(x).wait()
        cot_copy(x).wait()

        @pl.when(x + 2 < rows)
        def _():
            begin(x + 2)

    def use(x, g, first, space_ref):
        for c in range(first, first + PER_USE):
            o = g * CB + c
            for y in range(0, ny, YB):
                at = slice(y, y + YB)
                u = space_ref[g, at, c * nz : (c + 1) * nz] + local_ref[o, x, at, :].astype(F32)
                grad_ref[o, x, at, :] = (gelu_slope(u) * cot_ref[o, x, at, :].astype(F32)).astype(BF16)

    pair = rows_in_turn(rows, z_out_ref, b_ref, even_ref, odd_ref, arrive, use, lambda x: grad_copy(x).start())

    def block(h):
        lax.fori_loop(h * XB // 2, (h + 1) * XB // 2, pair, 0)
        analyse_y(
            lambda c: grad_ref[c, pl.ds(h * XB, XB)].reshape(XB * ny, nz), 0, channels, y_in_ref[...], g_ref
        )
        total = analyse_z(z_in_ref, g_ref)
        put_lines(out_ref, h, 0, total)

    each_row(rows // XB, block)
    each_row(rows, lambda x: grad_copy(x).wait())


def space_scratch(rows, channels, ny, nz):
    groups = channels // CB
    return [
        pltpu.VMEM((2 * KY * 2 * XB, KZ * channels), BF16),
        pltpu.VMEM((rows, groups, ny, 2 * KZ * CB), BF16),
        pltpu.VMEM((groups, ny, CB * nz), F32),
        pltpu.VMEM((groups, ny, CB * nz), F32),
    ]


def slope(lines, local, cotangent, biases):
    channels, rows, ny, nz = local.shape
    y_in, z_in, y_out, z_out = plane_tables(ny, nz)
    lanes = KZ * channels
    bias_lanes = jnp.where(jnp.arange(KZ)[None, :, None] == 0, biases.reshape(-1, 1, CB), 0.0).reshape(1, lanes)
    return pl.pallas_call(
        slope_kernel,
        in_specs=[in_vmem(), in_vmem(), in_hbm(), in_hbm()] + [in_vmem()] * 4,
        out_specs=[in_hbm(), in_vmem()],
        out_shape=[
            jax.ShapeDtypeStruct(local.shape, BF16),
            jax.ShapeDtypeStruct((KY, rows // XB, 2 * XB, lanes), F32),
        ],
        scratch_shapes=[pltpu.VMEM(local.shape, BF16)] * 3
        + space_scratch(rows, channels, ny, nz)
        + [pltpu.VMEM((channels // CB * KY * 2 * XB, CB * 2 * nz), BF16)]
        + [pltpu.SemaphoreType.DMA((rows,))] * 3,
        compiler_params=params(44),
        name="slope",
    )(bias_lanes, lines, local, cotangent, jnp.asarray(y_in), jnp.asarray(z_in), jnp.asarray(y_out), jnp.asarray(z_out))


def back_kernel(
    factor, apart, lines_ref, *refs
):
    sums_ref, refs = (refs[0], refs[1:]) if apart else (None, refs)
    (
        local_hbm, y_out_ref, z_out_ref, out_hbm, mix_ref, bias_ref,
        local_ref, out_ref, low_ref, b_ref, even_ref, odd_ref, local_sem, out_sem,
    ) = refs
    channels, rows, ny, nz = local_ref.shape
    local_copy = row_copy(local_hbm, local_ref, local_sem)
    out_copy = row_copy(out_ref, out_hbm, out_sem)
    each_row(3, lambda x: local_copy(x).start())
    synthesise_y(lines_ref, None, y_out_ref, low_ref, b_ref)
    wide = channels * channels // 8
    shared = sums_ref[...] if apart else lines_ref[:, :, :, low_ref.shape[1] :]
    total = jnp.sum(shared, axis=0) * factor
    mixing, biases = total[0, :, :wide], total[-1, :, total.shape[2] - wide :]
    mix_ref[...] = jnp.concatenate([mixing[:, c : c + channels] for c in range(0, wide, channels)], axis=0)
    bias_ref[...] = biases[:1, :channels]

    def arrive(x):
        local_copy(x).wait()

        @pl.when(x + 3 < rows)
        def _():
            local_copy(x + 3).start()

    def use(x, g, first, space_ref):
        for c in range(first, first + PER_USE):
            o = g * CB + c
            for y in range(0, ny, YB):
                at = slice(y, y + YB)
                u = space_ref[g, at, c * nz : (c + 1) * nz] + local_ref[o, x, at, :].astype(F32)
                out_ref[o, x, at, :] = u.astype(BF16)

    pair = rows_in_turn(rows, z_out_ref, b_ref, even_ref, odd_ref, arrive, use, lambda x: out_copy(x).start())
    lax.fori_loop(0, rows // 2, pair, 0)
    each_row(rows, lambda x: out_copy(x).wait())


def back(lines, sums, local, factor):
    apart = sums is not None
    channels, rows, ny, nz = local.shape
    _, _, y_out, z_out = plane_tables(ny, nz)
    return pl.pallas_call(
        functools.partial(back_kernel, factor, apart),
        in_specs=[in_vmem()] * (1 + apart) + [in_hbm(), in_vmem(), in_vmem()],
        out_specs=[in_hbm(), in_vmem(), in_vmem()],
        out_shape=[
            jax.ShapeDtypeStruct(local.shape, BF16),
            jax.ShapeDtypeStruct((channels, channels), F32),
            jax.ShapeDtypeStruct((1, channels), F32),
        ],
        scratch_shapes=[pltpu.VMEM(local.shape, BF16)] * 2
        + space_scratch(rows, channels, ny, nz)
        + [pltpu.SemaphoreType.DMA((rows,))] * 2,
        compiler_params=params(46),
        name="back",
    )(lines, *([sums] if apart else []), local, jnp.asarray(y_out), jnp.asarray(z_out))


def cell_sums_kernel(grad_ref, f_ref, dlines_ref, sums_ref, acc_ref):
    step = pl.program_id(0)
    channels, rows, ny, nz = f_ref.shape
    lanes = KZ * CB

    @pl.when(step == 0)
    def _():
        acc_ref[...] = jnp.zeros_like(acc_ref)

    def tiles(ref):
        return jnp.concatenate(
            [ref[:, x, y : y + YB, :].reshape(-1, nz) for x in range(rows) for y in range(0, ny, YB)], axis=1
        )

    acc_ref[...] += lax.dot_general(tiles(grad_ref), tiles(f_ref), (((1,), (1,)), ((), ())), preferred_element_type=F32)

    @pl.when(step == pl.num_programs(0) - 1)
    def _():
        n = channels * YB
        same = lax.rem(lax.broadcasted_iota(jnp.int32, (n, n), 0), YB) == lax.rem(
            lax.broadcasted_iota(jnp.int32, (n, n), 1), YB
        )
        picked = jnp.where(same, acc_ref[...], 0.0)
        fold = (
            lax.broadcasted_iota(jnp.int32, (channels, n), 1) // YB
            == lax.broadcasted_iota(jnp.int32, (channels, n), 0)
        ).astype(F32)
        half = exact_dot(fold, picked, ((1,), (0,)))
        mixing = exact_dot(half, fold, ((1,), (1,)))
        zero = dlines_ref[KY // 2].reshape(-1, KZ * channels)
        real = lax.rem(lax.broadcasted_iota(jnp.int32, (zero.shape[0], 1), 0), 2 * XB) < XB
        line = jnp.sum(jnp.where(real, zero, 0.0), axis=0, keepdims=True)
        lane = lax.broadcasted_iota(jnp.int32, (channels, KZ * channels), 1)
        channel = lax.broadcasted_iota(jnp.int32, (channels, KZ * channels), 0)
        pick = (lane == channel // CB * lanes + lax.rem(channel, CB)).astype(F32)
        biases = exact_dot(jnp.broadcast_to(line, (8, line.shape[1])), pick, ((1,), (1,)))
        packed = [
            jnp.concatenate([mixing[r : r + 8] for r in range(0, channels, 8)], axis=1),
            jnp.concatenate([biases] * (channels // 8), axis=1),
        ]
        if sums_ref.shape[0] == 1:
            sums_ref[0] = jnp.concatenate(packed, axis=1)
        else:
            for h in range(sums_ref.shape[0]):
                sums_ref[h] = packed[min(h, 1)]


def cell_sums(pre_grad, features, dlines):
    channels, rows, ny, nz = features.shape
    cells = pl.BlockSpec((channels, 2, ny, nz), lambda x: (0, x, 0, 0))
    tile = channels * YB
    blocks = rows // XB
    shape = (blocks, 8, channels * channels // 8 * (2 if blocks == 1 else 1))
    return pl.pallas_call(
        cell_sums_kernel,
        grid=(rows // 2,),
        in_specs=[cells, cells, whole(dlines.shape)],
        out_specs=whole(shape),
        out_shape=jax.ShapeDtypeStruct(shape, F32),
        scratch_shapes=[pltpu.VMEM((tile, tile), F32)],
        compiler_params=params(53),
        name="cell_sums",
    )(pre_grad, features, dlines)


def swap(blocks):
    return lax.all_to_all(blocks, "mp", 0, 0, tiled=True)


def shards(features, cotangent, spectral_weight, pointwise_weight, biases):
    channels, rows, ny, nz = features.shape
    devices = lax.axis_size("mp")
    nx = rows * devices
    pairs = spectral_weight.shape[0]
    groups = channels // CB
    blocks = rows // XB
    cut = KZ // pairs
    cells = nx * ny * nz
    x_in, x_out = line_tables(nx)
    if cut == 1:
        first_k = 0
    else:
        first_k = lax.rem(lax.axis_index("mp"), cut) * pairs
    ks = jnp.broadcast_to(jnp.arange(pairs)[None, :, None] + first_k, (groups, pairs, CB)).reshape(1, -1)
    scale = jnp.where(ks == 0, 1.0, 2.0).astype(F32) / float(cells)

    def to_owner(lines):
        if cut > 1:
            lines = lines.reshape(KY, blocks, 2 * XB, groups, cut, pairs * CB)
            lines = lines.transpose(0, 4, 1, 2, 3, 5)
        return swap(lines.reshape(devices, blocks, 2 * XB, -1))

    def to_cells(lines):
        lines = swap(lines)
        own = pairs * channels
        extra = None
        if cut > 1:
            extra = lines[..., own:]
            lines = lines[..., :own].reshape(KY, cut, blocks, 2 * XB, groups, pairs * CB)
            lines = lines.transpose(0, 2, 3, 4, 1, 5).reshape(KY, blocks, 2 * XB, -1)
        return lines, extra

    lines = to_owner(feature_lines(features))
    packed = pack_weights(spectral_weight)
    lines, packed = lax.optimization_barrier((lines, packed))
    mixed, spec = mix_modes(lines, packed, scale, x_in, x_out)
    pre_grad, dlines = slope(to_cells(mixed)[0], local_branch(features, pointwise_weight, False), cotangent, biases)
    sums = cell_sums(pre_grad, features, dlines)
    dlines = to_owner(dlines)
    dmixed, dspec = adjoint_modes(dlines, packed, scale, x_in, x_out, sums)
    back_lines, sums = to_cells(dmixed)
    spectral_grad = mode_gradient(spec, dspec)
    late_grad, _ = lax.optimization_barrier((pre_grad, dspec))
    local_back = local_branch(late_grad, pointwise_weight, True)
    features_grad, mix_total, bias_total = back(back_lines, sums, local_back, float(cells) ** -0.5)
    return (features_grad, spectral_grad, mix_total, bias_total[0])


def solution(mesh):
    return jax.shard_map(
        shards,
        mesh=mesh,
        in_specs=(
            P(None, ("groups", "mp"), None, None),
            P(None, ("groups", "mp"), None, None),
            P("mp", None, None, None, None),
            P(),
            P(),
        ),
        out_specs=(
            P(None, ("groups", "mp"), None, None),
            P(("groups", "mp"), None, None, None, None),
            P("groups", None),
            P("groups"),
        ),
        check_vma=False,
    )
```
